32 devices in a mesh: wide: 32 (over z, y, x, core), narrow: 1.
Axes of the slice: x: 2, y: 2, z: 4, core: 2. Of those that a mesh axis runs over, the one named last changes fastest.
Arguments:
- field: float32 [256, 44, 512], P('wide', 'narrow')
- sketch_one: float32 [512, 128], replicated, may hold values from -6 to 6
- sketch_two: float32 [256, 128], replicated, may hold values from -6 to 6
- ranks: int32 [2], replicated, may hold values from 64 to 128, as said below
Outputs:
- core: float32 [128, 44, 128], P('wide', 'narrow')
The draws below stay inside these ranges and needn't reach their ends.
Inputs may be any that keep to these rules, and one draw needn't show every extreme that they name: One of the two ranks equals 128.
All inputs are finite; a program needn't handle non-finite values.
Results may differ from the reference program's by a relative error of at most 0.00022.
Values sent between devices are 32-bit elements; how exact they have to be, the bound alone decides.
A program may use at most 64 MiB of HBM per device.

```python
import math
import jax
import jax.numpy as jnp
from jax import lax

N1 = 512
Y_DEV = 8
Z_DEV = 4
C = 11
RMAX = 128
N2 = 256
N3 = 4


def draw_field(key, part):
    keys = jax.random.split(jax.random.fold_in(key, 11), 6)
    total = N3 * C
    spread = 3.0
    mixing = 0.6
    base = jax.random.normal(keys[2], (N1, N2, total), jnp.float32)
    first = jax.random.normal(keys[3], (N1 // 4, 1, N2, total), jnp.float32)
    second = jax.random.normal(keys[4], (N1, N2 // 4, 1, total), jnp.float32)
    row_scale = jnp.exp(jax.random.uniform(keys[0], (N1, 1, 1), jnp.float32) * math.log(spread))
    col_scale = jnp.exp(jax.random.uniform(keys[1], (1, N2, 1), jnp.float32) * math.log(spread))
    mixed = (base.reshape(N1 // 4, 4, N2, total) + mixing * first).reshape(N1, N2, total)
    mixed = (mixed.reshape(N1, N2 // 4, 4, total) + mixing * second).reshape(N1, N2, total)
    scaled = row_scale * col_scale * mixed / math.sqrt(1.0 + 2.0 * mixing * mixing)
    narrow_count = N3 // Z_DEV
    owners = N2 // Y_DEV * narrow_count
    joint = (jnp.arange(N2) // Y_DEV)[:, None] * narrow_count + (jnp.arange(total) // (Z_DEV * C))[None, :]
    paired = jax.random.permutation(keys[5], N1)
    owned = paired[joint % N1]
    heavy = jnp.arange(N1)[:, None, None] == owned[None, :, :]
    boost = math.sqrt(2.0 * owners)
    scaled = jnp.where(heavy, boost * scaled, scaled)
    return jnp.transpose(scaled, (1, 2, 0)).astype(jnp.float32)


def draw_ranks(key, part):
    keys = jax.random.split(jax.random.fold_in(key, 23), 2)
    which = jax.random.randint(keys[0], (), 0, 2)
    other = jax.random.randint(keys[1], (), RMAX // 2, RMAX + 1)
    return jnp.where(jnp.arange(2) == which, RMAX, other).astype(jnp.int32)


def gaussian(own_key, extent, deviation, most, held_as=jnp.bfloat16):
    return jnp.clip(deviation * jax.random.normal(own_key, extent, jnp.float32), -most, most).astype(held_as)


def setup_inputs(seed: int = 0) -> dict:
    seeds = jax.random.split(jax.random.key(seed), 5)
    return {
        "field": draw_field(jax.random.fold_in(seeds[4], 71), 0),
        "sketch_one": gaussian(seeds[1], (N1, RMAX), 1.0, 6.0, jnp.float32),
        "sketch_two": gaussian(seeds[2], (N2, RMAX), 1.0, 6.0, jnp.float32),
        "ranks": draw_ranks(jax.random.fold_in(seeds[4], 71), 0),
    }


def make_basis(gram, sketch, rank):
    keep = (jnp.arange(sketch.shape[1]) < rank).astype(jnp.float32)
    sketched = jnp.dot(gram, sketch * keep, precision=lax.Precision.HIGHEST)
    inner = jnp.dot(sketched.T, sketched, precision=lax.Precision.HIGHEST) + jnp.diag(1.0 - keep)
    lower = jnp.linalg.cholesky(inner)
    return jax.scipy.linalg.solve_triangular(lower, sketched.T, lower=True)

def reference(field, sketch_one, sketch_two, ranks):
    highest = lax.Precision.HIGHEST
    gram_one = jnp.einsum('ykn,ykm->nm', field, field, precision=highest)
    basis_one = make_basis(gram_one, sketch_one, ranks[0])
    core_one = jnp.einsum('rn,ykn->rky', basis_one, field, precision=highest)
    gram_two = jnp.einsum('rkn,rkm->nm', core_one, core_one, precision=highest)
    basis_two = make_basis(gram_two, sketch_two, ranks[1])
    return jnp.einsum('sn,rkn->rks', basis_two, core_one, precision=highest)
```

```python
import functools

import jax
import jax.numpy as jnp
from jax import lax
from jax.experimental import pallas as pl
from jax.experimental.pallas import tpu as pltpu
from jax.sharding import PartitionSpec as P

HIGHEST = lax.Precision.HIGHEST
MESH = pl.DeviceIdType.MESH


def make_basis(local, sketch, rank):
    keep = (jnp.arange(sketch.shape[1]) < rank).astype(jnp.float32)
    masked = sketch * keep
    part = jnp.einsum("akn,ns->aks", local, masked, precision=HIGHEST)
    part = jnp.einsum("akn,aks->ns", local, part, precision=HIGHEST)
    sketched = lax.psum(part, ("wide", "narrow"))
    inner = jnp.dot(sketched.T, sketched, precision=HIGHEST) + jnp.diag(1.0 - keep)
    lower = jnp.linalg.cholesky(inner)
    return jax.scipy.linalg.solve_triangular(lower, sketched.T, lower=True)


def general(field, sketch_one, sketch_two, ranks):
    basis_one = make_basis(field, sketch_one, ranks[0])
    core_one = jnp.einsum("rn,ykn->rky", basis_one, field, precision=HIGHEST)
    regrouped = lax.all_to_all(core_one, "wide", split_axis=0, concat_axis=2, tiled=True)
    basis_two = make_basis(regrouped, sketch_two, ranks[1])
    return jnp.einsum("sn,rkn->rks", basis_two, regrouped, precision=HIGHEST)


def dot(a, b, dims):
    return lax.dot_general(
        a, b, (dims, ((), ())), precision=HIGHEST, preferred_element_type=jnp.float32
    )


NN = ((1,), (0,))
NT = ((1,), (1,))
TN = ((0,), (0,))
BLOCK = 8
TILES = 4
KB = 2
PLANE = 8
USED = 6


def inverse_factor(work, linv):
    size = linv.shape[0]
    tile = (BLOCK, size)
    group = TILES * BLOCK
    sub = lax.broadcasted_iota(jnp.int32, tile, 0)

    for r0 in range(0, size, group):
        own = work[r0 : r0 + group, :size]
        rest = work[r0 : r0 + group, size:]
        rows_a = [own[u * BLOCK : (u + 1) * BLOCK, :] for u in range(TILES)]
        rows_t = [rest[u * BLOCK : (u + 1) * BLOCK, :] for u in range(TILES)]
        panels_a, panels_t = [], []
        for u in range(TILES):
            d, below = {}, {}
            for q in range(BLOCK):
                lane = r0 + u * BLOCK + q
                column = jnp.broadcast_to(rows_a[u][:, lane : lane + 1], tile)
                for p in range(q, BLOCK):
                    d[p, q] = jnp.broadcast_to(column[p : p + 1, :], tile)
                for v in range(u + 1, TILES):
                    below[v, q] = jnp.broadcast_to(rows_a[v][:, lane : lane + 1], tile)
            done_a, done_t = [], []
            panel_a = jnp.zeros(tile, jnp.float32)
            panel_t = jnp.zeros(tile, jnp.float32)
            for j in range(BLOCK):
                x = d[j, j]
                y = lax.rsqrt(x)
                y = y * (1.5 - 0.5 * ((x * y) * y))
                for p in range(j + 1, BLOCK):
                    d[p, j] = d[p, j] * y
                for v in range(u + 1, TILES):
                    below[v, j] = below[v, j] * y
                for q in range(j + 1, BLOCK):
                    for p in range(q, BLOCK):
                        d[p, q] = d[p, q] - d[p, j] * d[q, j]
                    for v in range(u + 1, TILES):
                        below[v, q] = below[v, q] - below[v, j] * d[q, j]
                ra = jnp.broadcast_to(rows_a[u][j : j + 1, :], tile)
                rt = jnp.broadcast_to(rows_t[u][j : j + 1, :], tile)
                for k in range(j):
                    ra = ra - d[j, k] * done_a[k]
                    rt = rt - d[j, k] * done_t[k]
                ra = ra * y
                rt = rt * y
                done_a.append(ra)
                done_t.append(rt)
                panel_a = jnp.where(sub == j, ra, panel_a)
                panel_t = jnp.where(sub == j, rt, panel_t)
                for v in range(u + 1, TILES):
                    rows_a[v] = rows_a[v] - below[v, j] * ra
                    rows_t[v] = rows_t[v] - below[v, j] * rt
            panels_a.append(panel_a)
            panels_t.append(panel_t)
        panel_t = jnp.concatenate(panels_t, axis=0)
        panel_a = jnp.concatenate(panels_a, axis=0)
        linv[r0 : r0 + group, :] = panel_t
        end = r0 + group
        if end < size:
            both = jnp.concatenate([panel_a, panel_t], axis=1)
            work[end:, :] = work[end:, :] - dot(panel_a.T[end:, :], both, NN)


def fill_work(work, inner, keep_row, size):
    row = lax.broadcasted_iota(jnp.int32, (size, size), 0)
    col = lax.broadcasted_iota(jnp.int32, (size, size), 1)
    eye = (row == col).astype(jnp.float32)
    work[:, :size] = inner + eye * (1.0 - keep_row)
    work[:, size:] = eye


def far_first(bits, low):
    def hops(m):
        flat = sum((m >> b) & 1 for b in range(low))
        return flat + (m >> low)

    return sorted(range(1, 1 << bits), key=lambda m: -hops(m))


def kernel(
    n, field, sketch_one, sketch_two, ranks_in, out,
    flat, s1, s2, ranks, part, pair, mine, got, full, rot, have, work, linv, stack,
    part_two, pair_two, mine_two, got_two, full_two, give, last,
    load_sem, send_sem, recv_sem,
):
    me = lax.axis_index("wide")
    size = s1.shape[1]
    wide = flat.shape[2]
    holders = rot.shape[0] // KB
    ydev = rot.shape[1]
    n2 = s2.shape[0]
    per = size // n
    chips = n // 2
    rows = size // chips
    core = lax.rem(me, 2)
    chip = me // 2

    loads = [
        pltpu.make_async_copy(ranks_in, ranks, load_sem.at[0]),
        pltpu.make_async_copy(sketch_one, s1, load_sem.at[1]),
        pltpu.make_async_copy(field.at[:, pl.ds(0, wide)], flat.at[0], load_sem.at[2]),
        pltpu.make_async_copy(field.at[:, pl.ds(wide, wide)], flat.at[1], load_sem.at[3]),
        pltpu.make_async_copy(sketch_two, s2, load_sem.at[4]),
    ]
    for load in loads:
        load.start()

    barrier = pltpu.get_barrier_semaphore()

    def greet(i, carry):
        peer = lax.rem(me + 1 + i, n)
        pl.semaphore_signal(barrier, inc=1, device_id={"wide": peer}, device_id_type=MESH)
        return carry

    lax.fori_loop(0, n - 1, greet, 0)

    bits = n.bit_length() - 1
    deltas = [(1 - 2 * lax.rem(me // (1 << b), 2)) * (1 << b) for b in range(bits)]

    def flipped(m):
        return me + sum(deltas[b] for b in range(bits) if (m >> b) & 1)

    alike = [(2 * m, flipped(2 * m)) for m in far_first(bits - 1, 2)]
    every = [(m, flipped(m)) for m in far_first(bits, 3)]
    twin = flipped(1)

    def copy(phase, source, target, peer):
        return pltpu.make_async_remote_copy(
            src_ref=source, dst_ref=target,
            send_sem=send_sem.at[phase], recv_sem=recv_sem.at[phase],
            device_id={"wide": peer}, device_id_type=MESH,
        )

    def of_chip(c):
        return pl.ds(pl.multiple_of(c * rows, rows), rows)

    slot = (me // PLANE) * USED + lax.rem(me, PLANE)
    holds = jnp.logical_and(lax.rem(me, PLANE) < USED, slot < holders)
    idle = jnp.logical_not(holds)

    loads[0].wait()
    lane = lax.broadcasted_iota(jnp.int32, (1, size), 1)
    sub = lax.broadcasted_iota(jnp.int32, (size, 1), 0)
    keep_one = (lane < ranks[0]).astype(jnp.float32)
    keep_two = (lane < ranks[1]).astype(jnp.float32)
    loads[1].wait()
    turned = s1[...].T * (sub < ranks[0]).astype(jnp.float32)
    loads[2].wait()
    projected = dot(turned[:, :wide], flat[0], NT)
    loads[3].wait()
    projected = projected + dot(turned[:, wide:], flat[1], NT)
    part[1 - core] = dot(projected, flat[1 - core], NN)

    pl.semaphore_wait(barrier, n - 1)

    copy(0, part.at[1 - core], pair, twin).start()
    part[core] = dot(projected, flat[core], NN)
    copy(0, pair, pair, twin).wait_recv()
    mine[...] = part[core] + pair[...]
    for i, (m, peer) in enumerate(alike):
        copy(1, mine.at[of_chip(peer // 2), :], got.at[m // 2 - 1], peer).start()
    loads[4].wait()
    masked_two = (s2[...].T) * (sub < ranks[1]).astype(jnp.float32)
    s2t = masked_two
    copy(1, got, got, twin).wait_recv()
    full[core, of_chip(chip), :] = jnp.sum(got[...], axis=0) + mine[of_chip(chip), :]
    for m, peer in alike:
        own = full.at[core, of_chip(chip), :]
        copy(2, own, own, peer).start()
    copy(2, got, got, twin).wait_recv()
    copy(3, full.at[core], full.at[core], twin).start()
    sk = full[core]
    turn = dot(flat[core], sk, NT)
    inner = dot(sk, sk, NT)
    copy(3, pair, pair, twin).wait_recv()
    sk = full[1 - core]
    turn = turn + dot(flat[1 - core], sk, NT)
    rot[...] = turn.reshape(rot.shape)

    mine_y = pl.ds(pl.multiple_of(me * ydev, ydev), ydev)
    planes = n // PLANE
    plane = me // PLANE
    for t in range(planes):
        far = planes - 1 - t
        there = plane + sum(
            (deltas[3 + b] // PLANE) for b in range(bits - 3) if (far >> b) & 1
        )
        for i in range(USED):
            inside = lax.rem(lax.rem(me, PLANE) + 1 + i, USED)
            j = there * USED + inside
            peer = there * PLANE + inside

            @pl.when(jnp.logical_and(j < holders, peer != me))
            def _():
                copy(
                    4, rot.at[pl.ds(KB * j, KB)], have.at[:, mine_y, :], peer
                ).start()

    @pl.when(holds)
    def _():
        have[:, mine_y, :] = rot[pl.ds(KB * slot, KB)]

    inner = inner + dot(sk, sk, NT)
    fill_work(work, inner, keep_one, size)
    inverse_factor(work, linv)

    half_two = n2 // 2
    holder_chips = holders // 2

    @pl.when(holds)
    def _():
        everything = have.at[:, pl.ds(0, n2 - ydev), :]
        copy(4, everything, everything, twin).wait_recv()
        for k in range(KB):
            stack[k * size : (k + 1) * size, :] = dot(linv[...], have[k], NT)
        mixed = stack[...]
        spread = dot(s2t, mixed, NT)
        total = dot(spread, mixed, NN)
        part_two[0] = total[:, :half_two]
        part_two[1] = total[:, half_two:]
        copy(5, part_two.at[1 - core], pair_two, twin).start()
        copy(5, pair_two, pair_two, twin).wait_recv()
        mine_two[...] = part_two[core] + pair_two[...]
        for m, peer in alike:
            copy(
                6, mine_two.at[of_chip(peer // 2), :], got_two.at[slot // 2], peer
            ).start()
        got_two[slot // 2] = mine_two[of_chip(chip), :]
        all_but_one = got_two.at[pl.ds(0, holder_chips - 1)]
        copy(6, all_but_one, all_but_one, twin).wait_recv()

    @pl.when(idle)
    def _():
        copy(6, got_two, got_two, twin).wait_recv()

    lanes = pl.ds(pl.multiple_of(core * half_two, half_two), half_two)
    own = full_two.at[of_chip(chip), lanes]
    own[...] = jnp.sum(got_two[...], axis=0)
    for m, peer in every:
        copy(7, own, own, peer).start()
    others = give.at[pl.ds(0, n - 1)]
    copy(7, others, others, twin).wait_recv()

    sk = full_two[...]
    low = lax.broadcasted_iota(jnp.int32, (KB * per, size), 0) < per

    @pl.when(holds)
    def _():
        spun = dot(stack[...], full_two[...], NT)
        for t in range(n // 2):
            first = spun[KB * per * t : KB * per * (t + 1), :]
            second = spun[size + KB * per * t : size + KB * per * (t + 1), :]
            give[2 * t] = jnp.where(low, first, pltpu.roll(second, per, 0))
            give[2 * t + 1] = jnp.where(low, pltpu.roll(first, per, 0), second)
        for m, peer in every:
            copy(8, give.at[peer], last.at[slot], peer).start()
        last[slot] = give[me]

    fill_work(work, dot(sk, sk, NT), keep_two, size)
    inverse_factor(work, linv)

    @pl.when(holds)
    def _():
        most = last.at[pl.ds(0, holders - 1)]
        copy(8, most, most, twin).wait_recv()

    @pl.when(idle)
    def _():
        copy(8, last, last, twin).wait_recv()

    out[...] = dot(last[...].reshape(out.shape), linv[...], NT)

    copy(0, pair, pair, twin).wait_send()
    copy(1, got, got, twin).wait_send()
    copy(2, got, got, twin).wait_send()
    copy(3, pair, pair, twin).wait_send()
    copy(7, others, others, twin).wait_send()

    @pl.when(holds)
    def _():
        most = rot.at[pl.ds(0, KB * (holders - 1))]
        copy(4, most, most, twin).wait_send()
        copy(5, pair_two, pair_two, twin).wait_send()
        most = mine_two.at[pl.ds(0, size - rows), :]
        copy(6, most, most, twin).wait_send()
        most = give.at[pl.ds(0, n - 1)]
        copy(8, most, most, twin).wait_send()

    @pl.when(idle)
    def _():
        copy(4, rot, rot, twin).wait_send()


def fused(n, field, sketch_one, sketch_two, ranks):
    ydev, kdim, n1 = field.shape
    n2, size = sketch_two.shape
    chips = n // 2
    rows = size // chips
    wide = n1 // 2
    holders = kdim // KB
    per = size // n
    hbm = pl.BlockSpec(memory_space=pltpu.MemorySpace.HBM)
    f32 = jnp.float32
    lines = jnp.transpose(field, (1, 0, 2)).reshape(kdim * ydev, n1)
    core = pl.pallas_call(
        functools.partial(kernel, n),
        out_shape=jax.ShapeDtypeStruct((kdim * per, size), f32),
        in_specs=[hbm, hbm, hbm, hbm],
        out_specs=pl.BlockSpec(memory_space=pltpu.VMEM),
        scratch_shapes=[
            pltpu.VMEM((2, kdim * ydev, wide), f32),
            pltpu.VMEM((n1, size), f32),
            pltpu.VMEM((n2, size), f32),
            pltpu.SMEM((2,), jnp.int32),
            pltpu.VMEM((2, size, wide), f32),
            pltpu.VMEM((size, wide), f32),
            pltpu.VMEM((size, wide), f32),
            pltpu.VMEM((chips - 1, rows, wide), f32),
            pltpu.VMEM((2, size, wide), f32),
            pltpu.VMEM((kdim, ydev, size), f32),
            pltpu.VMEM((KB, n2, size), f32),
            pltpu.VMEM((size, 2 * size), f32),
            pltpu.VMEM((size, size), f32),
            pltpu.VMEM((KB * size, n2), f32),
            pltpu.VMEM((2, size, n2 // 2), f32),
            pltpu.VMEM((size, n2 // 2), f32),
            pltpu.VMEM((size, n2 // 2), f32),
            pltpu.VMEM((holders // 2, rows, n2 // 2), f32),
            pltpu.VMEM((size, n2), f32),
            pltpu.VMEM((n, KB * per, size), f32),
            pltpu.VMEM((holders, KB * per, size), f32),
            pltpu.SemaphoreType.DMA((5,)),
            pltpu.SemaphoreType.DMA((9,)),
            pltpu.SemaphoreType.DMA((9,)),
        ],
        compiler_params=pltpu.CompilerParams(
            collective_id=0, has_side_effects=True, vmem_limit_bytes=56 * 1024 * 1024
        ),
        cost_estimate=pl.CostEstimate(
            flops=600_000_000, bytes_accessed=2_000_000, transcendentals=256
        ),
    )(lines, sketch_one, sketch_two, ranks)
    return jnp.transpose(core.reshape(kdim, per, size), (1, 0, 2))


def solution(mesh):
    n = mesh.shape["wide"]

    def per_device(field, sketch_one, sketch_two, ranks):
        ydev, kdim, n1 = field.shape
        n2, size = sketch_two.shape
        fits = (
            mesh.shape["narrow"] == 1
            and size == 128
            and n == 32
            and ydev == 8
            and kdim % (2 * KB) == 0
            and kdim // KB <= n // PLANE * USED
            and n1 == 512
            and n2 == 8 * n
        )
        if fits:
            return fused(n, field, sketch_one, sketch_two, ranks)
        return general(field, sketch_one, sketch_two, ranks)

    return jax.shard_map(
        per_device,
        mesh=mesh,
        in_specs=(P("wide", "narrow", None), P(), P(), P()),
        out_specs=P("wide", "narrow", None),
        check_vma=False,
    )
```

```python
import functools

import jax
import jax.numpy as jnp
from jax import lax
from jax.experimental import pallas as pl
from jax.experimental.pallas import tpu as pltpu
from jax.sharding import PartitionSpec as P

HIGHEST = lax.Precision.HIGHEST
MESH = pl.DeviceIdType.MESH


def make_basis(local, sketch, rank):
    keep = (jnp.arange(sketch.shape[1]) < rank).astype(jnp.float32)
    masked = sketch * keep
    part = jnp.einsum("akn,ns->aks", local, masked, precision=HIGHEST)
    part = jnp.einsum("akn,aks->ns", local, part, precision=HIGHEST)
    sketched = lax.psum(part, ("wide", "narrow"))
    inner = jnp.dot(sketched.T, sketched, precision=HIGHEST) + jnp.diag(1.0 - keep)
    lower = jnp.linalg.cholesky(inner)
    return jax.scipy.linalg.solve_triangular(lower, sketched.T, lower=True)


def general(field, sketch_one, sketch_two, ranks):
    basis_one = make_basis(field, sketch_one, ranks[0])
    core_one = jnp.einsum("rn,ykn->rky", basis_one, field, precision=HIGHEST)
    regrouped = lax.all_to_all(core_one, "wide", split_axis=0, concat_axis=2, tiled=True)
    basis_two = make_basis(regrouped, sketch_two, ranks[1])
    return jnp.einsum("sn,rkn->rks", basis_two, regrouped, precision=HIGHEST)


def dot(a, b, dims):
    return lax.dot_general(
        a, b, (dims, ((), ())), precision=HIGHEST, preferred_element_type=jnp.float32
    )


NN = ((1,), (0,))
NT = ((1,), (1,))
TN = ((0,), (0,))
BLOCK = 8
TILES = 4
KB = 3
PLANE = 8


def inverse_factor(work, linv):
    size = linv.shape[0]
    tile = (BLOCK, size)
    group = TILES * BLOCK
    sub = lax.broadcasted_iota(jnp.int32, tile, 0)

    for r0 in range(0, size, group):
        own = work[r0 : r0 + group, :size]
        rest = work[r0 : r0 + group, size:]
        rows_a = [own[u * BLOCK : (u + 1) * BLOCK, :] for u in range(TILES)]
        rows_t = [rest[u * BLOCK : (u + 1) * BLOCK, :] for u in range(TILES)]
        panels_a, panels_t = [], []
        for u in range(TILES):
            d, below = {}, {}
            for q in range(BLOCK):
                lane = r0 + u * BLOCK + q
                column = jnp.broadcast_to(rows_a[u][:, lane : lane + 1], tile)
                for p in range(q, BLOCK):
                    d[p, q] = jnp.broadcast_to(column[p : p + 1, :], tile)
                for v in range(u + 1, TILES):
                    below[v, q] = jnp.broadcast_to(rows_a[v][:, lane : lane + 1], tile)
            done_a, done_t = [], []
            panel_a = jnp.zeros(tile, jnp.float32)
            panel_t = jnp.zeros(tile, jnp.float32)
            for j in range(BLOCK):
                x = d[j, j]
                y = lax.rsqrt(x)
                y = y * (1.5 - 0.5 * ((x * y) * y))
                for p in range(j + 1, BLOCK):
                    d[p, j] = d[p, j] * y
                for v in range(u + 1, TILES):
                    below[v, j] = below[v, j] * y
                for q in range(j + 1, BLOCK):
                    for p in range(q, BLOCK):
                        d[p, q] = d[p, q] - d[p, j] * d[q, j]
                    for v in range(u + 1, TILES):
                        below[v, q] = below[v, q] - below[v, j] * d[q, j]
                ra = jnp.broadcast_to(rows_a[u][j : j + 1, :], tile)
                rt = jnp.broadcast_to(rows_t[u][j : j + 1, :], tile)
                for k in range(j):
                    ra = ra - d[j, k] * done_a[k]
                    rt = rt - d[j, k] * done_t[k]
                ra = ra * y
                rt = rt * y
                done_a.append(ra)
                done_t.append(rt)
                panel_a = jnp.where(sub == j, ra, panel_a)
                panel_t = jnp.where(sub == j, rt, panel_t)
                for v in range(u + 1, TILES):
                    rows_a[v] = rows_a[v] - below[v, j] * ra
                    rows_t[v] = rows_t[v] - below[v, j] * rt
            panels_a.append(panel_a)
            panels_t.append(panel_t)
        panel_t = jnp.concatenate(panels_t, axis=0)
        panel_a = jnp.concatenate(panels_a, axis=0)
        linv[r0 : r0 + group, :] = panel_t
        end = r0 + group
        if end < size:
            both = jnp.concatenate([panel_a, panel_t], axis=1)
            work[end:, :] = work[end:, :] - dot(panel_a.T[end:, :], both, NN)


def fill_work(work, inner, keep_row, size):
    row = lax.broadcasted_iota(jnp.int32, (size, size), 0)
    col = lax.broadcasted_iota(jnp.int32, (size, size), 1)
    eye = (row == col).astype(jnp.float32)
    work[:, :size] = inner + eye * (1.0 - keep_row)
    work[:, size:] = eye


def far_first(bits, low):
    def hops(m):
        flat = sum((m >> b) & 1 for b in range(low))
        return flat + (m >> low)

    return sorted(range(1, 1 << bits), key=lambda m: -hops(m))


def kernel(
    n, field, sketch_one, sketch_two, ranks_in, out,
    flat, s1, s2, ranks, part, pair, mine, got, full, rot, have, work, linv, stack,
    part_two, got_two, full_two, give, last,
    load_sem, send_sem, recv_sem,
):
    me = lax.axis_index("wide")
    size = s1.shape[1]
    wide = flat.shape[2]
    holders = last.shape[0]
    lines = field.shape[0]
    ydev = rot.shape[1]
    n2 = s2.shape[0]
    per = size // n
    chips = n // 2
    rows = size // chips
    core = lax.rem(me, 2)
    chip = me // 2

    loads = [
        pltpu.make_async_copy(ranks_in, ranks, load_sem.at[0]),
        pltpu.make_async_copy(sketch_one, s1, load_sem.at[1]),
    ] + [
        pltpu.make_async_copy(
            field.at[:, pl.ds(wide * h, wide)],
            flat.at[h, pl.ds(0, lines), :],
            load_sem.at[2 + h],
        )
        for h in range(2)
    ] + [
        pltpu.make_async_copy(sketch_two, s2, load_sem.at[4]),
    ]
    for load in loads:
        load.start()

    barrier = pltpu.get_barrier_semaphore()

    def greet(i, carry):
        peer = lax.rem(me + 1 + i, n)
        pl.semaphore_signal(barrier, inc=1, device_id={"wide": peer}, device_id_type=MESH)
        return carry

    lax.fori_loop(0, n - 1, greet, 0)

    bits = n.bit_length() - 1
    deltas = [(1 - 2 * lax.rem(me // (1 << b), 2)) * (1 << b) for b in range(bits)]

    def flipped(m):
        return me + sum(deltas[b] for b in range(bits) if (m >> b) & 1)

    alike = [(2 * m, flipped(2 * m)) for m in far_first(bits - 1, 2)]
    twin = flipped(1)

    def copy(phase, source, target, peer):
        return pltpu.make_async_remote_copy(
            src_ref=source, dst_ref=target,
            send_sem=send_sem.at[phase], recv_sem=recv_sem.at[phase],
            device_id={"wide": peer}, device_id_type=MESH,
        )

    waits = []

    def later(phase, sent, when=None):
        def wait():
            copy(phase, sent, sent, twin).wait_send()

        waits.append(wait if when is None else functools.partial(pl.when(when), wait))

    def of_chip(c):
        return pl.ds(pl.multiple_of(c * rows, rows), rows)

    plane = me // PLANE
    below = me - plane * PLANE
    middle = jnp.logical_or(plane == 1, plane == 2)
    outside = jnp.logical_not(middle)
    slot = jnp.clip(me - PLANE, 0, 2 * PLANE - 1)
    holds = jnp.logical_and(middle, slot < holders)
    spare = jnp.logical_not(holds)
    turns = (6, 7, 4, 5, 2, 3, 1, 0)
    inside = [below + sum(deltas[b] for b in range(3) if (m >> b) & 1) for m in turns]
    nearer = jnp.where(plane < 2, PLANE, 2 * PLANE)
    farther = 3 * PLANE - nearer
    group = [b + farther for b in inside] + [b + nearer for b in inside[:-1]]
    edges = [b + 3 * (farther - PLANE) for b in inside] + [
        b + 3 * (nearer - PLANE) for b in inside
    ]

    for h in range(2):
        flat[h, lines:, :] = jnp.zeros((flat.shape[1] - lines, wide), jnp.float32)
    loads[0].wait()
    lane = lax.broadcasted_iota(jnp.int32, (1, size), 1)
    sub = lax.broadcasted_iota(jnp.int32, (size, 1), 0)
    keep_one = (lane < ranks[0]).astype(jnp.float32)
    keep_two = (lane < ranks[1]).astype(jnp.float32)
    loads[1].wait()
    turned = s1[...].T * (sub < ranks[0]).astype(jnp.float32)
    loads[2].wait()
    projected = dot(turned[:, :wide], flat[0, :lines, :], NT)
    loads[3].wait()
    projected = projected + dot(turned[:, wide:], flat[1, :lines, :], NT)
    part[1 - core] = dot(projected, flat[1 - core, pl.ds(0, lines), :], NN)

    pl.semaphore_wait(barrier, n - 1)
    copy(0, part.at[1 - core], pair, twin).start()
    later(0, pair)
    part[core] = dot(projected, flat[core, pl.ds(0, lines), :], NN)
    copy(0, pair, pair, twin).wait_recv()
    mine[...] = part[core] + pair[...]
    for i, (m, peer) in enumerate(alike):
        copy(1, mine.at[of_chip(peer // 2), :], got.at[m // 2 - 1], peer).start()
    later(1, got)
    loads[4].wait()
    masked_two = (s2[...].T) * (sub < ranks[1]).astype(jnp.float32)
    s2t = masked_two
    copy(1, got, got, twin).wait_recv()
    full[core, of_chip(chip), :] = jnp.sum(got[...], axis=0) + mine[of_chip(chip), :]
    for m, peer in alike:
        own = full.at[core, of_chip(chip), :]
        copy(2, own, own, peer).start()
    later(2, got)
    copy(2, got, got, twin).wait_recv()
    copy(3, full.at[core], full.at[core], twin).start()
    later(3, pair)
    sk = full[core]
    rot[...] = dot(flat[core], sk, NT).reshape(rot.shape)
    inner = dot(sk, sk, NT)
    copy(3, pair, pair, twin).wait_recv()
    sk = full[1 - core]

    mine_y = pl.ds(pl.multiple_of(me * ydev, ydev), ydev)
    part_lines = PLANE * KB * ydev
    for base in (farther, nearer):
        first = base - PLANE
        ks = pl.ds(KB * first, KB * PLANE)
        span = pl.ds(pl.multiple_of(first * (KB * ydev), part_lines), part_lines)
        more = dot(flat[1 - core, span, :], sk, NT)
        rot[ks] = rot[ks] + more.reshape(KB * PLANE, ydev, size)
        for b in inside:
            peer = b + base
            j = peer - PLANE

            @pl.when(jnp.logical_and(j < holders, peer != me))
            def _():
                copy(
                    4, rot.at[pl.ds(KB * j, KB)], have.at[:, mine_y, :], peer
                ).start()

    later(4, rot.at[pl.ds(0, KB * (holders - 1))], holds)
    later(4, rot.at[pl.ds(0, KB * holders)], spare)

    @pl.when(holds)
    def _():
        have[:, mine_y, :] = rot[pl.ds(KB * slot, KB)]

    inner = inner + dot(sk, sk, NT)
    fill_work(work, inner, keep_one, size)
    inverse_factor(work, linv)

    @pl.when(holds)
    def _():
        everything = have.at[:, pl.ds(0, n2 - ydev), :]
        copy(4, everything, everything, twin).wait_recv()

    @pl.when(holds)
    def _():
        for k in range(KB):
            stack[k * size : (k + 1) * size, :] = dot(linv[...], have[k], NT)
        mixed = stack[...]
        spread = dot(s2t, mixed, NT)
        total = dot(spread, mixed, NN)
        part_two[...] = total

    def of_slot(j):
        return pl.ds(pl.multiple_of(j * rows, rows), rows)

    @pl.when(holds)
    def _():
        for peer in group:
            copy(6, part_two.at[of_slot(peer - PLANE), :], got_two.at[slot], peer).start()
        got_two[slot] = part_two[of_slot(slot), :]
        most = got_two.at[pl.ds(0, holders - 1)]
        copy(6, most, most, twin).wait_recv()

    @pl.when(jnp.logical_and(middle, spare))
    def _():
        copy(6, got_two, got_two, twin).wait_recv()

    later(6, part_two.at[pl.ds(0, size - rows), :], holds)
    most_two = full_two.at[pl.ds(0, size - rows), :]

    @pl.when(middle)
    def _():
        own = full_two.at[of_slot(slot), :]
        own[...] = jnp.sum(got_two[...], axis=0)
        for peer in group:
            copy(7, own, own, peer).start()
        for peer in edges:
            copy(5, own, own, peer).start()
        copy(7, most_two, most_two, twin).wait_recv()

    @pl.when(outside)
    def _():
        copy(5, full_two, full_two, twin).wait_recv()

    later(7, most_two, middle)
    later(5, full_two, middle)

    @pl.when(holds)
    def _():
        spun = dot(stack[...], full_two[...], NT)
        for d in range(n):
            for k in range(KB):
                give[d, k] = spun[k * size + per * d : k * size + per * (d + 1), :]
        for peer in edges + group:
            copy(8, give.at[peer], last.at[slot], peer).start()
        last[slot] = give[me]

    later(8, give.at[pl.ds(0, n - 1)], holds)
    sk = full_two[...]
    fill_work(work, dot(sk, sk, NT), keep_two, size)
    inverse_factor(work, linv)

    @pl.when(holds)
    def _():
        most = last.at[pl.ds(0, holders - 1)]
        copy(8, most, most, twin).wait_recv()

    @pl.when(spare)
    def _():
        copy(8, last, last, twin).wait_recv()

    done = dot(last[...].reshape(holders * KB * per, size), linv[...], NT)
    out[...] = done[: out.shape[0], :]

    for wait in waits:
        wait()


def fused(n, field, sketch_one, sketch_two, ranks):
    ydev, kdim, n1 = field.shape
    n2, size = sketch_two.shape
    chips = n // 2
    rows = size // chips
    wide = n1 // 2
    holders = -(-kdim // KB)
    padded = 2 * PLANE * KB
    per = size // n
    hbm = pl.BlockSpec(memory_space=pltpu.MemorySpace.HBM)
    f32 = jnp.float32
    lines = jnp.transpose(field, (1, 0, 2)).reshape(kdim * ydev, n1)
    core = pl.pallas_call(
        functools.partial(kernel, n),
        out_shape=jax.ShapeDtypeStruct((kdim * per, size), f32),
        in_specs=[hbm, hbm, hbm, hbm],
        out_specs=pl.BlockSpec(memory_space=pltpu.VMEM),
        scratch_shapes=[
            pltpu.VMEM((2, padded * ydev, wide), f32),
            pltpu.VMEM((n1, size), f32),
            pltpu.VMEM((n2, size), f32),
            pltpu.SMEM((2,), jnp.int32),
            pltpu.VMEM((2, size, wide), f32),
            pltpu.VMEM((size, wide), f32),
            pltpu.VMEM((size, wide), f32),
            pltpu.VMEM((chips - 1, rows, wide), f32),
            pltpu.VMEM((2, size, wide), f32),
            pltpu.VMEM((padded, ydev, size), f32),
            pltpu.VMEM((KB, n2, size), f32),
            pltpu.VMEM((size, 2 * size), f32),
            pltpu.VMEM((size, size), f32),
            pltpu.VMEM((KB * size, n2), f32),
            pltpu.VMEM((size, n2), f32),
            pltpu.VMEM((holders, rows, n2), f32),
            pltpu.VMEM((size, n2), f32),
            pltpu.VMEM((n, KB, per, size), f32),
            pltpu.VMEM((holders, KB, per, size), f32),
            pltpu.SemaphoreType.DMA((5,)),
            pltpu.SemaphoreType.DMA((9,)),
            pltpu.SemaphoreType.DMA((9,)),
        ],
        compiler_params=pltpu.CompilerParams(
            collective_id=0, has_side_effects=True, vmem_limit_bytes=55075 * 1024
        ),
        cost_estimate=pl.CostEstimate(
            flops=600_000_000, bytes_accessed=2_000_000, transcendentals=256
        ),
    )(lines, sketch_one, sketch_two, ranks)
    return jnp.transpose(core.reshape(kdim, per, size), (1, 0, 2))


def solution(mesh):
    n = mesh.shape["wide"]

    def per_device(field, sketch_one, sketch_two, ranks):
        ydev, kdim, n1 = field.shape
        n2, size = sketch_two.shape
        fits = (
            mesh.shape["narrow"] == 1
            and size == 128
            and n == 32
            and ydev == 8
            and kdim <= 2 * PLANE * KB - KB
            and kdim > 2 * PLANE * KB - 2 * KB
            and n1 == 512
            and n2 == 8 * n
        )
        if fits:
            return fused(n, field, sketch_one, sketch_two, ranks)
        return general(field, sketch_one, sketch_two, ranks)

    return jax.shard_map(
        per_device,
        mesh=mesh,
        in_specs=(P("wide", "narrow", None), P(), P(), P()),
        out_specs=P("wide", "narrow", None),
        check_vma=False,
    )
```

```python
import functools

import jax
import jax.numpy as jnp
from jax import lax
from jax.experimental import pallas as pl
from jax.experimental.pallas import tpu as pltpu
from jax.sharding import PartitionSpec as P

HIGHEST = lax.Precision.HIGHEST
MESH = pl.DeviceIdType.MESH


def make_basis(local, sketch, rank):
    keep = (jnp.arange(sketch.shape[1]) < rank).astype(jnp.float32)
    masked = sketch * keep
    part = jnp.einsum("akn,ns->aks", local, masked, precision=HIGHEST)
    part = jnp.einsum("akn,aks->ns", local, part, precision=HIGHEST)
    sketched = lax.psum(part, ("wide", "narrow"))
    inner = jnp.dot(sketched.T, sketched, precision=HIGHEST) + jnp.diag(1.0 - keep)
    lower = jnp.linalg.cholesky(inner)
    return jax.scipy.linalg.solve_triangular(lower, sketched.T, lower=True)


def general(field, sketch_one, sketch_two, ranks):
    basis_one = make_basis(field, sketch_one, ranks[0])
    core_one = jnp.einsum("rn,ykn->rky", basis_one, field, precision=HIGHEST)
    regrouped = lax.all_to_all(core_one, "wide", split_axis=0, concat_axis=2, tiled=True)
    basis_two = make_basis(regrouped, sketch_two, ranks[1])
    return jnp.einsum("sn,rkn->rks", basis_two, regrouped, precision=HIGHEST)


def dot(a, b, dims):
    return lax.dot_general(
        a, b, (dims, ((), ())), precision=HIGHEST, preferred_element_type=jnp.float32
    )


def halves(x):
    high = x.astype(jnp.bfloat16)
    return high, (x - high.astype(jnp.float32)).astype(jnp.bfloat16)


def mul(a, b, dims):
    def one(x, y):
        return lax.dot_general(
            x, y, (dims, ((), ())), preferred_element_type=jnp.float32
        )

    (ah, al), (bh, bl) = halves(a), halves(b)
    return one(ah, bh) + (one(ah, bl) + one(al, bh))


NN = ((1,), (0,))
NT = ((1,), (1,))
TN = ((0,), (0,))
BLOCK = 8
TILES = 8
KB = 3
PLANE = 8


def inverse_factor(work, linv):
    size = linv.shape[0]
    tile = (BLOCK, size)
    group = TILES * BLOCK
    sub = lax.broadcasted_iota(jnp.int32, tile, 0)

    for r0 in range(0, size, group):
        own = work[r0 : r0 + group, :size]
        rest = work[r0 : r0 + group, size:]
        rows_a = [own[u * BLOCK : (u + 1) * BLOCK, :] for u in range(TILES)]
        rows_t = [rest[u * BLOCK : (u + 1) * BLOCK, :] for u in range(TILES)]
        panels_a, panels_t = [], []
        for u in range(TILES):
            d, below = {}, {}
            for q in range(BLOCK):
                lane = r0 + u * BLOCK + q
                column = jnp.broadcast_to(rows_a[u][:, lane : lane + 1], tile)
                for p in range(q, BLOCK):
                    d[p, q] = jnp.broadcast_to(column[p : p + 1, :], tile)
                for v in range(u + 1, TILES):
                    below[v, q] = jnp.broadcast_to(rows_a[v][:, lane : lane + 1], tile)
            m = {}
            done_a, done_t = [], []
            panel_a = jnp.zeros(tile, jnp.float32)
            panel_t = jnp.zeros(tile, jnp.float32)
            for j in range(BLOCK):
                x = d[j, j]
                r = 1.0 / x
                y = lax.rsqrt(x)
                for q in range(j + 1, BLOCK):
                    for p in range(q, BLOCK):
                        d[p, q] = d[p, q] - (d[p, j] * d[q, j]) * r
                for p in range(j + 1, BLOCK):
                    m[p, j] = d[p, j] * r
                low = {}
                for v in range(u + 1, TILES):
                    low[v] = below[v, j] * r
                    for q in range(j + 1, BLOCK):
                        below[v, q] = below[v, q] - low[v] * d[q, j]
                ra = jnp.broadcast_to(rows_a[u][j : j + 1, :], tile)
                rt = jnp.broadcast_to(rows_t[u][j : j + 1, :], tile)
                for k in range(j):
                    ra = ra - m[j, k] * done_a[k]
                    rt = rt - m[j, k] * done_t[k]
                done_a.append(ra)
                done_t.append(rt)
                panel_a = jnp.where(sub == j, ra * y, panel_a)
                panel_t = jnp.where(sub == j, rt * y, panel_t)
                for v in range(u + 1, TILES):
                    rows_a[v] = rows_a[v] - low[v] * ra
                    rows_t[v] = rows_t[v] - low[v] * rt
            panels_a.append(panel_a)
            panels_t.append(panel_t)
        panel_t = jnp.concatenate(panels_t, axis=0)
        panel_a = jnp.concatenate(panels_a, axis=0)
        linv[r0 : r0 + group, :] = panel_t
        end = r0 + group
        if end < size:
            both = jnp.concatenate([panel_a, panel_t], axis=1)
            work[end:, :] = work[end:, :] - dot(panel_a.T[end:, :], both, NN)


def fill_work(work, inner, keep_row, size):
    row = lax.broadcasted_iota(jnp.int32, (size, size), 0)
    col = lax.broadcasted_iota(jnp.int32, (size, size), 1)
    eye = (row == col).astype(jnp.float32)
    work[:, :size] = inner + eye * (1.0 - keep_row)
    work[:, size:] = eye


def far_first(bits, low):
    def hops(m):
        flat = sum((m >> b) & 1 for b in range(low))
        return flat + (m >> low)

    return sorted(range(1, 1 << bits), key=lambda m: -hops(m))


def kernel(
    n, field, sketch_one, sketch_two, ranks_in, out,
    flat, s1, s2, ranks, part, pair, mine, got, full, rot, have, work, linv, stack,
    part_two, got_two, full_two, give, last,
    load_sem, send_sem, recv_sem,
):
    me = lax.axis_index("wide")
    size = s1.shape[1]
    wide = flat.shape[2]
    holders = last.shape[0]
    lines = field.shape[0]
    ydev = rot.shape[1]
    n2 = s2.shape[0]
    per = size // n
    chips = n // 2
    rows = size // chips
    core = lax.rem(me, 2)
    chip = me // 2

    loads = [
        pltpu.make_async_copy(ranks_in, ranks, load_sem.at[0]),
        pltpu.make_async_copy(sketch_one, s1, load_sem.at[1]),
    ] + [
        pltpu.make_async_copy(
            field.at[:, pl.ds(wide * h, wide)],
            flat.at[h, pl.ds(0, lines), :],
            load_sem.at[2 + h],
        )
        for h in range(2)
    ] + [
        pltpu.make_async_copy(sketch_two, s2, load_sem.at[4]),
    ]
    for load in loads:
        load.start()

    barrier = pltpu.get_barrier_semaphore()

    def greet(i, carry):
        peer = lax.rem(me + 1 + i, n)
        pl.semaphore_signal(barrier, inc=1, device_id={"wide": peer}, device_id_type=MESH)
        return carry

    lax.fori_loop(0, n - 1, greet, 0)

    bits = n.bit_length() - 1
    deltas = [(1 - 2 * lax.rem(me // (1 << b), 2)) * (1 << b) for b in range(bits)]

    def flipped(m):
        return me + sum(deltas[b] for b in range(bits) if (m >> b) & 1)

    alike = [(2 * m, flipped(2 * m)) for m in far_first(bits - 1, 2)]
    twin = flipped(1)

    def copy(phase, source, target, peer):
        return pltpu.make_async_remote_copy(
            src_ref=source, dst_ref=target,
            send_sem=send_sem.at[phase], recv_sem=recv_sem.at[phase],
            device_id={"wide": peer}, device_id_type=MESH,
        )

    waits = []

    def later(phase, sent, when=None):
        def wait():
            copy(phase, sent, sent, twin).wait_send()

        waits.append(wait if when is None else functools.partial(pl.when(when), wait))

    def of_chip(c):
        return pl.ds(pl.multiple_of(c * rows, rows), rows)

    plane = me // PLANE
    below = me - plane * PLANE
    middle = jnp.logical_or(plane == 1, plane == 2)
    outside = jnp.logical_not(middle)
    slot = jnp.clip(me - PLANE, 0, 2 * PLANE - 1)
    holds = jnp.logical_and(middle, slot < holders)
    spare = jnp.logical_not(holds)
    turns = (6, 7, 4, 5, 2, 3, 1, 0)
    inside = [below + sum(deltas[b] for b in range(3) if (m >> b) & 1) for m in turns]
    nearer = jnp.where(plane < 2, PLANE, 2 * PLANE)
    farther = 3 * PLANE - nearer
    group = [b + farther for b in inside] + [b + nearer for b in inside[:-1]]
    edges = [b + 3 * (farther - PLANE) for b in inside] + [
        b + 3 * (nearer - PLANE) for b in inside
    ]

    for h in range(2):
        flat[h, lines:, :] = jnp.zeros((flat.shape[1] - lines, wide), jnp.float32)
    loads[0].wait()
    lane = lax.broadcasted_iota(jnp.int32, (1, size), 1)
    sub = lax.broadcasted_iota(jnp.int32, (size, 1), 0)
    keep_one = (lane < ranks[0]).astype(jnp.float32)
    keep_two = (lane < ranks[1]).astype(jnp.float32)
    loads[1].wait()
    turned = s1[...].T * (sub < ranks[0]).astype(jnp.float32)
    loads[2].wait()
    projected = mul(turned[:, :wide], flat[0, :lines, :], NT)
    loads[3].wait()
    projected = projected + mul(turned[:, wide:], flat[1, :lines, :], NT)
    part[1 - core] = mul(projected, flat[1 - core, pl.ds(0, lines), :], NN)

    pl.semaphore_wait(barrier, n - 1)
    copy(0, part.at[1 - core], pair, twin).start()
    later(0, pair)
    part[core] = mul(projected, flat[core, pl.ds(0, lines), :], NN)
    copy(0, pair, pair, twin).wait_recv()
    mine[...] = part[core] + pair[...]
    for i, (m, peer) in enumerate(alike):
        copy(1, mine.at[of_chip(peer // 2), :], got.at[m // 2 - 1], peer).start()
    later(1, got)
    loads[4].wait()
    masked_two = (s2[...].T) * (sub < ranks[1]).astype(jnp.float32)
    s2t = masked_two
    copy(1, got, got, twin).wait_recv()
    full[core, of_chip(chip), :] = jnp.sum(got[...], axis=0) + mine[of_chip(chip), :]
    for m, peer in alike:
        own = full.at[core, of_chip(chip), :]
        copy(2, own, own, peer).start()
    later(2, got)
    copy(2, got, got, twin).wait_recv()
    copy(3, full.at[core], full.at[core], twin).start()
    later(3, pair)
    sk = full[core]
    rot[...] = mul(flat[core], sk, NT).reshape(rot.shape)
    inner = dot(sk, sk, NT)
    copy(3, pair, pair, twin).wait_recv()
    sk = full[1 - core]

    mine_y = pl.ds(pl.multiple_of(me * ydev, ydev), ydev)
    part_lines = PLANE * KB * ydev
    for base in (farther, nearer):
        first = base - PLANE
        ks = pl.ds(KB * first, KB * PLANE)
        span = pl.ds(pl.multiple_of(first * (KB * ydev), part_lines), part_lines)
        more = mul(flat[1 - core, span, :], sk, NT)
        rot[ks] = rot[ks] + more.reshape(KB * PLANE, ydev, size)
        for b in inside:
            peer = b + base
            j = peer - PLANE

            @pl.when(jnp.logical_and(j < holders, peer != me))
            def _():
                copy(
                    4, rot.at[pl.ds(KB * j, KB)], have.at[:, mine_y, :], peer
                ).start()

    later(4, rot.at[pl.ds(0, KB * (holders - 1))], holds)
    later(4, rot.at[pl.ds(0, KB * holders)], spare)

    @pl.when(holds)
    def _():
        have[:, mine_y, :] = rot[pl.ds(KB * slot, KB)]

    inner = inner + dot(sk, sk, NT)
    fill_work(work, inner, keep_one, size)
    inverse_factor(work, linv)

    @pl.when(holds)
    def _():
        everything = have.at[:, pl.ds(0, n2 - ydev), :]
        copy(4, everything, everything, twin).wait_recv()

    @pl.when(holds)
    def _():
        for k in range(KB):
            stack[k * size : (k + 1) * size, :] = mul(linv[...], have[k], NT)
        mixed = stack[...]
        spread = mul(s2t, mixed, NT)
        total = mul(spread, mixed, NN)
        part_two[...] = total

    def of_slot(j):
        place = lax.rem(j, 2) * PLANE + j // 2
        return pl.ds(pl.multiple_of(place * rows, rows), rows)

    @pl.when(holds)
    def _():
        for peer in group:
            copy(6, part_two.at[of_slot(peer - PLANE), :], got_two.at[slot], peer).start()
        got_two[slot] = part_two[of_slot(slot), :]
        most = got_two.at[pl.ds(0, holders - 1)]
        copy(6, most, most, twin).wait_recv()

    @pl.when(jnp.logical_and(middle, spare))
    def _():
        copy(6, got_two, got_two, twin).wait_recv()

    later(6, part_two.at[pl.ds(0, size - rows), :], holds)
    most_two = full_two.at[pl.ds(0, size - rows), :]

    @pl.when(middle)
    def _():
        own = full_two.at[of_slot(slot), :]
        own[...] = jnp.sum(got_two[...], axis=0)
        for peer in group:
            copy(7, own, own, peer).start()
        for peer in edges:
            copy(5, own, own, peer).start()
        copy(7, most_two, most_two, twin).wait_recv()

    @pl.when(outside)
    def _():
        copy(5, full_two, full_two, twin).wait_recv()

    later(7, most_two, middle)
    later(5, full_two, middle)

    @pl.when(holds)
    def _():
        spun = mul(stack[...], full_two[...], NT)
        for d in range(n):
            for k in range(KB):
                give[d, k] = spun[k * size + per * d : k * size + per * (d + 1), :]
        for peer in edges + group:
            copy(8, give.at[peer], last.at[slot], peer).start()
        last[slot] = give[me]

    later(8, give.at[pl.ds(0, n - 1)], holds)
    sk = full_two[...]
    fill_work(work, mul(sk, sk, NT), keep_two, size)
    inverse_factor(work, linv)

    @pl.when(holds)
    def _():
        most = last.at[pl.ds(0, holders - 1)]
        copy(8, most, most, twin).wait_recv()

    @pl.when(spare)
    def _():
        copy(8, last, last, twin).wait_recv()

    done = mul(last[...].reshape(holders * KB * per, size), linv[...], NT)
    out[...] = done[: out.shape[0], :]

    for wait in waits:
        wait()


def fused(n, field, sketch_one, sketch_two, ranks):
    ydev, kdim, n1 = field.shape
    n2, size = sketch_two.shape
    chips = n // 2
    rows = size // chips
    wide = n1 // 2
    holders = -(-kdim // KB)
    padded = 2 * PLANE * KB
    per = size // n
    hbm = pl.BlockSpec(memory_space=pltpu.MemorySpace.HBM)
    f32 = jnp.float32
    lines = jnp.transpose(field, (1, 0, 2)).reshape(kdim * ydev, n1)
    core = pl.pallas_call(
        functools.partial(kernel, n),
        out_shape=pltpu.VMEM((kdim * per, size), f32),
        in_specs=[hbm, hbm, hbm, hbm],
        out_specs=pl.BlockSpec(memory_space=pltpu.VMEM),
        scratch_shapes=[
            pltpu.VMEM((2, padded * ydev, wide), f32),
            pltpu.VMEM((n1, size), f32),
            pltpu.VMEM((n2, size), f32),
            pltpu.SMEM((2,), jnp.int32),
            pltpu.VMEM((2, size, wide), f32),
            pltpu.VMEM((size, wide), f32),
            pltpu.VMEM((size, wide), f32),
            pltpu.VMEM((chips - 1, rows, wide), f32),
            pltpu.VMEM((2, size, wide), f32),
            pltpu.VMEM((padded, ydev, size), f32),
            pltpu.VMEM((KB, n2, size), f32),
            pltpu.VMEM((size, 2 * size), f32),
            pltpu.VMEM((size, size), f32),
            pltpu.VMEM((KB * size, n2), f32),
            pltpu.VMEM((size, n2), f32),
            pltpu.VMEM((holders, rows, n2), f32),
            pltpu.VMEM((size, n2), f32),
            pltpu.VMEM((n, KB, per, size), f32),
            pltpu.VMEM((holders, KB, per, size), f32),
            pltpu.SemaphoreType.DMA((5,)),
            pltpu.SemaphoreType.DMA((9,)),
            pltpu.SemaphoreType.DMA((9,)),
        ],
        compiler_params=pltpu.CompilerParams(
            collective_id=0, has_side_effects=True, vmem_limit_bytes=56 * 1024 * 1024
        ),
        cost_estimate=pl.CostEstimate(
            flops=600_000_000, bytes_accessed=2_000_000, transcendentals=256
        ),
    )(lines, sketch_one, sketch_two, ranks)
    return jnp.transpose(core.reshape(kdim, per, size), (1, 0, 2))


def solution(mesh):
    n = mesh.shape["wide"]

    def per_device(field, sketch_one, sketch_two, ranks):
        ydev, kdim, n1 = field.shape
        n2, size = sketch_two.shape
        fits = (
            mesh.shape["narrow"] == 1
            and size == 128
            and n == 32
            and ydev == 8
            and kdim <= 2 * PLANE * KB - KB
            and kdim > 2 * PLANE * KB - 2 * KB
            and n1 == 512
            and n2 == 8 * n
        )
        if fits:
            return fused(n, field, sketch_one, sketch_two, ranks)
        return general(field, sketch_one, sketch_two, ranks)

    return jax.shard_map(
        per_device,
        mesh=mesh,
        in_specs=(P("wide", "narrow", None), P(), P(), P()),
        out_specs=P("wide", "narrow", None),
        check_vma=False,
    )
```

```python
import functools

import jax
import jax.numpy as jnp
from jax import lax
from jax.experimental import pallas as pl
from jax.experimental.pallas import tpu as pltpu
from jax.sharding import PartitionSpec as P

HIGHEST = lax.Precision.HIGHEST
MESH = pl.DeviceIdType.MESH


def make_basis(local, sketch, rank):
    keep = (jnp.arange(sketch.shape[1]) < rank).astype(jnp.float32)
    masked = sketch * keep
    part = jnp.einsum("akn,ns->aks", local, masked, precision=HIGHEST)
    part = jnp.einsum("akn,aks->ns", local, part, precision=HIGHEST)
    sketched = lax.psum(part, ("wide", "narrow"))
    inner = jnp.dot(sketched.T, sketched, precision=HIGHEST) + jnp.diag(1.0 - keep)
    lower = jnp.linalg.cholesky(inner)
    return jax.scipy.linalg.solve_triangular(lower, sketched.T, lower=True)


def general(field, sketch_one, sketch_two, ranks):
    basis_one = make_basis(field, sketch_one, ranks[0])
    core_one = jnp.einsum("rn,ykn->rky", basis_one, field, precision=HIGHEST)
    regrouped = lax.all_to_all(core_one, "wide", split_axis=0, concat_axis=2, tiled=True)
    basis_two = make_basis(regrouped, sketch_two, ranks[1])
    return jnp.einsum("sn,rkn->rks", basis_two, regrouped, precision=HIGHEST)


def dot(a, b, dims):
    return lax.dot_general(
        a, b, (dims, ((), ())), precision=HIGHEST, preferred_element_type=jnp.float32
    )


def halves(x):
    high = x.astype(jnp.bfloat16)
    return high, (x - high.astype(jnp.float32)).astype(jnp.bfloat16)


def mul(a, b, dims):
    def one(x, y):
        return lax.dot_general(
            x, y, (dims, ((), ())), preferred_element_type=jnp.float32
        )

    (ah, al), (bh, bl) = halves(a), halves(b)
    return one(ah, bh) + (one(ah, bl) + one(al, bh))


NN = ((1,), (0,))
NT = ((1,), (1,))
TN = ((0,), (0,))
BLOCK = 8
TILES = 8
KB = 3
PLANE = 8


def inverse_factor(work, linv):
    size = linv.shape[0]
    tile = (BLOCK, size)
    group = TILES * BLOCK
    sub = lax.broadcasted_iota(jnp.int32, tile, 0)

    for r0 in range(0, size, group):
        own = work[r0 : r0 + group, :size]
        rest = work[r0 : r0 + group, size:]
        rows_a = [own[u * BLOCK : (u + 1) * BLOCK, :] for u in range(TILES)]
        rows_t = [rest[u * BLOCK : (u + 1) * BLOCK, :] for u in range(TILES)]
        panels_a, panels_t = [], []
        ahead = None
        for u in range(TILES):
            d, below = {}, {}
            for q in range(BLOCK):
                lane = r0 + u * BLOCK + q
                if ahead is None:
                    column = jnp.broadcast_to(rows_a[u][:, lane : lane + 1], tile)
                else:
                    column = ahead[q]
                for p in range(q, BLOCK):
                    d[p, q] = jnp.broadcast_to(column[p : p + 1, :], tile)
                for v in range(u + 1, TILES):
                    below[v, q] = jnp.broadcast_to(rows_a[v][:, lane : lane + 1], tile)
            ahead = None
            if u + 1 < TILES:
                first = r0 + (u + 1) * BLOCK
                ahead = [
                    jnp.broadcast_to(rows_a[u + 1][:, first + q : first + q + 1], tile)
                    for q in range(BLOCK)
                ]
            m = {}
            done_a, done_t = [], []
            panel_a = jnp.zeros(tile, jnp.float32)
            panel_t = jnp.zeros(tile, jnp.float32)
            for j in range(BLOCK):
                x = d[j, j]
                r = 1.0 / x
                y = lax.rsqrt(x)
                for q in range(j + 1, BLOCK):
                    for p in range(q, BLOCK):
                        d[p, q] = d[p, q] - (d[p, j] * d[q, j]) * r
                for p in range(j + 1, BLOCK):
                    m[p, j] = d[p, j] * r
                low = {}
                for v in range(u + 1, TILES):
                    low[v] = below[v, j] * r
                    if v == u + 1:
                        for q in range(BLOCK):
                            across = jnp.broadcast_to(below[v, j][q : q + 1, :], tile)
                            ahead[q] = ahead[q] - low[v] * across
                    for q in range(j + 1, BLOCK):
                        below[v, q] = below[v, q] - low[v] * d[q, j]
                ra = jnp.broadcast_to(rows_a[u][j : j + 1, :], tile)
                rt = jnp.broadcast_to(rows_t[u][j : j + 1, :], tile)
                for k in range(j):
                    ra = ra - m[j, k] * done_a[k]
                    rt = rt - m[j, k] * done_t[k]
                done_a.append(ra)
                done_t.append(rt)
                panel_a = jnp.where(sub == j, ra * y, panel_a)
                panel_t = jnp.where(sub == j, rt * y, panel_t)
                for v in range(u + 1, TILES):
                    rows_a[v] = rows_a[v] - low[v] * ra
                    rows_t[v] = rows_t[v] - low[v] * rt
            panels_a.append(panel_a)
            panels_t.append(panel_t)
        panel_t = jnp.concatenate(panels_t, axis=0)
        panel_a = jnp.concatenate(panels_a, axis=0)
        linv[r0 : r0 + group, :] = panel_t
        end = r0 + group
        if end < size:
            both = jnp.concatenate([panel_a, panel_t], axis=1)
            work[end:, :] = work[end:, :] - dot(panel_a.T[end:, :], both, NN)


def fill_work(work, inner, keep_row, size):
    row = lax.broadcasted_iota(jnp.int32, (size, size), 0)
    col = lax.broadcasted_iota(jnp.int32, (size, size), 1)
    eye = (row == col).astype(jnp.float32)
    work[:, :size] = inner + eye * (1.0 - keep_row)
    work[:, size:] = eye


def far_first(bits, low):
    def hops(m):
        flat = sum((m >> b) & 1 for b in range(low))
        return flat + (m >> low)

    return sorted(range(1, 1 << bits), key=lambda m: -hops(m))


def kernel(
    n, field, sketch_one, sketch_two, ranks_in, out,
    flat, s1, s2, ranks, part, pair, mine, got, full, rot, have, work, linv, stack,
    part_two, got_two, full_two, give, last,
    load_sem, send_sem, recv_sem,
):
    me = lax.axis_index("wide")
    size = s1.shape[1]
    wide = flat.shape[2]
    holders = last.shape[0]
    lines = field.shape[0]
    ydev = rot.shape[1]
    n2 = s2.shape[0]
    per = size // n
    chips = n // 2
    rows = size // chips
    core = lax.rem(me, 2)
    chip = me // 2

    loads = [
        pltpu.make_async_copy(ranks_in, ranks, load_sem.at[0]),
        pltpu.make_async_copy(sketch_one, s1, load_sem.at[1]),
    ] + [
        pltpu.make_async_copy(
            field.at[:, pl.ds(wide * h, wide)],
            flat.at[h, pl.ds(0, lines), :],
            load_sem.at[2 + h],
        )
        for h in range(2)
    ] + [
        pltpu.make_async_copy(sketch_two, s2, load_sem.at[4]),
    ]
    for load in loads:
        load.start()

    barrier = pltpu.get_barrier_semaphore()

    def greet(i, carry):
        peer = lax.rem(me + 1 + i, n)
        pl.semaphore_signal(barrier, inc=1, device_id={"wide": peer}, device_id_type=MESH)
        return carry

    lax.fori_loop(0, n - 1, greet, 0)

    bits = n.bit_length() - 1
    deltas = [(1 - 2 * lax.rem(me // (1 << b), 2)) * (1 << b) for b in range(bits)]

    def flipped(m):
        return me + sum(deltas[b] for b in range(bits) if (m >> b) & 1)

    alike = [(2 * m, flipped(2 * m)) for m in far_first(bits - 1, 2)]
    twin = flipped(1)

    def copy(phase, source, target, peer):
        return pltpu.make_async_remote_copy(
            src_ref=source, dst_ref=target,
            send_sem=send_sem.at[phase], recv_sem=recv_sem.at[phase],
            device_id={"wide": peer}, device_id_type=MESH,
        )

    waits = []

    def later(phase, sent, when=None):
        def wait():
            copy(phase, sent, sent, twin).wait_send()

        waits.append(wait if when is None else functools.partial(pl.when(when), wait))

    def of_chip(c):
        return pl.ds(pl.multiple_of(c * rows, rows), rows)

    plane = me // PLANE
    below = me - plane * PLANE
    middle = jnp.logical_or(plane == 1, plane == 2)
    outside = jnp.logical_not(middle)
    slot = jnp.clip(me - PLANE, 0, 2 * PLANE - 1)
    holds = jnp.logical_and(middle, slot < holders)
    spare = jnp.logical_not(holds)
    turns = (6, 7, 4, 5, 2, 3, 1, 0)
    inside = [below + sum(deltas[b] for b in range(3) if (m >> b) & 1) for m in turns]
    nearer = jnp.where(plane < 2, PLANE, 2 * PLANE)
    farther = 3 * PLANE - nearer
    group = [b + farther for b in inside] + [b + nearer for b in inside[:-1]]
    edges = [b + 3 * (farther - PLANE) for b in inside] + [
        b + 3 * (nearer - PLANE) for b in inside
    ]

    for h in range(2):
        flat[h, lines:, :] = jnp.zeros((flat.shape[1] - lines, wide), jnp.float32)
    loads[0].wait()
    lane = lax.broadcasted_iota(jnp.int32, (1, size), 1)
    sub = lax.broadcasted_iota(jnp.int32, (size, 1), 0)
    keep_one = (lane < ranks[0]).astype(jnp.float32)
    keep_two = (lane < ranks[1]).astype(jnp.float32)
    loads[1].wait()
    turned = s1[...].T * (sub < ranks[0]).astype(jnp.float32)
    loads[2].wait()
    projected = mul(turned[:, :wide], flat[0, :lines, :], NT)
    loads[3].wait()
    projected = projected + mul(turned[:, wide:], flat[1, :lines, :], NT)
    part[1 - core] = mul(projected, flat[1 - core, pl.ds(0, lines), :], NN)

    pl.semaphore_wait(barrier, n - 1)
    copy(0, part.at[1 - core], pair, twin).start()
    later(0, pair)
    part[core] = mul(projected, flat[core, pl.ds(0, lines), :], NN)
    copy(0, pair, pair, twin).wait_recv()
    mine[...] = part[core] + pair[...]
    for i, (m, peer) in enumerate(alike):
        copy(1, mine.at[of_chip(peer // 2), :], got.at[m // 2 - 1], peer).start()
    later(1, got)
    loads[4].wait()
    masked_two = (s2[...].T) * (sub < ranks[1]).astype(jnp.float32)
    s2t = masked_two
    copy(1, got, got, twin).wait_recv()
    full[core, of_chip(chip), :] = jnp.sum(got[...], axis=0) + mine[of_chip(chip), :]
    for m, peer in alike:
        own = full.at[core, of_chip(chip), :]
        copy(2, own, own, peer).start()
    later(2, got)
    copy(2, got, got, twin).wait_recv()
    copy(3, full.at[core], full.at[core], twin).start()
    later(3, pair)
    sk = full[core]
    rot[...] = mul(flat[core], sk, NT).reshape(rot.shape)
    inner = dot(sk, sk, NT)
    copy(3, pair, pair, twin).wait_recv()
    sk = full[1 - core]

    mine_y = pl.ds(pl.multiple_of(me * ydev, ydev), ydev)
    part_lines = PLANE * KB * ydev
    for base in (farther, nearer):
        first = base - PLANE
        ks = pl.ds(KB * first, KB * PLANE)
        span = pl.ds(pl.multiple_of(first * (KB * ydev), part_lines), part_lines)
        more = mul(flat[1 - core, span, :], sk, NT)
        rot[ks] = rot[ks] + more.reshape(KB * PLANE, ydev, size)
        for b in inside:
            peer = b + base
            j = peer - PLANE

            @pl.when(jnp.logical_and(j < holders, peer != me))
            def _():
                copy(
                    4, rot.at[pl.ds(KB * j, KB)], have.at[:, mine_y, :], peer
                ).start()

    later(4, rot.at[pl.ds(0, KB * (holders - 1))], holds)
    later(4, rot.at[pl.ds(0, KB * holders)], spare)

    @pl.when(holds)
    def _():
        have[:, mine_y, :] = rot[pl.ds(KB * slot, KB)]

    inner = inner + dot(sk, sk, NT)
    fill_work(work, inner, keep_one, size)
    inverse_factor(work, linv)

    @pl.when(holds)
    def _():
        everything = have.at[:, pl.ds(0, n2 - ydev), :]
        copy(4, everything, everything, twin).wait_recv()

    @pl.when(holds)
    def _():
        for k in range(KB):
            stack[k * size : (k + 1) * size, :] = mul(linv[...], have[k], NT)
        mixed = stack[...]
        spread = mul(s2t, mixed, NT)
        total = mul(spread, mixed, NN)
        part_two[...] = total

    def of_slot(j):
        place = lax.rem(j, 2) * PLANE + j // 2
        return pl.ds(pl.multiple_of(place * rows, rows), rows)

    @pl.when(holds)
    def _():
        for peer in group:
            copy(6, part_two.at[of_slot(peer - PLANE), :], got_two.at[slot], peer).start()
        got_two[slot] = part_two[of_slot(slot), :]
        most = got_two.at[pl.ds(0, holders - 1)]
        copy(6, most, most, twin).wait_recv()

    @pl.when(jnp.logical_and(middle, spare))
    def _():
        copy(6, got_two, got_two, twin).wait_recv()

    later(6, part_two.at[pl.ds(0, size - rows), :], holds)
    most_two = full_two.at[pl.ds(0, size - rows), :]

    @pl.when(middle)
    def _():
        own = full_two.at[of_slot(slot), :]
        own[...] = jnp.sum(got_two[...], axis=0)
        for peer in group:
            copy(7, own, own, peer).start()
        for peer in edges:
            copy(5, own, own, peer).start()
        copy(7, most_two, most_two, twin).wait_recv()

    @pl.when(outside)
    def _():
        copy(5, full_two, full_two, twin).wait_recv()

    later(7, most_two, middle)
    later(5, full_two, middle)

    @pl.when(holds)
    def _():
        spun = mul(stack[...], full_two[...], NT)
        for d in range(n):
            for k in range(KB):
                give[d, k] = spun[k * size + per * d : k * size + per * (d + 1), :]
        for peer in edges + group:
            copy(8, give.at[peer], last.at[slot], peer).start()
        last[slot] = give[me]

    later(8, give.at[pl.ds(0, n - 1)], holds)
    sk = full_two[...]
    fill_work(work, mul(sk, sk, NT), keep_two, size)
    inverse_factor(work, linv)

    @pl.when(holds)
    def _():
        most = last.at[pl.ds(0, holders - 1)]
        copy(8, most, most, twin).wait_recv()

    @pl.when(spare)
    def _():
        copy(8, last, last, twin).wait_recv()

    done = mul(last[...].reshape(holders * KB * per, size), linv[...], NT)
    out[...] = done[: out.shape[0], :]

    for wait in waits:
        wait()


def fused(n, field, sketch_one, sketch_two, ranks):
    ydev, kdim, n1 = field.shape
    n2, size = sketch_two.shape
    chips = n // 2
    rows = size // chips
    wide = n1 // 2
    holders = -(-kdim // KB)
    padded = 2 * PLANE * KB
    per = size // n
    hbm = pl.BlockSpec(memory_space=pltpu.MemorySpace.HBM)
    f32 = jnp.float32
    lines = jnp.transpose(field, (1, 0, 2)).reshape(kdim * ydev, n1)
    core = pl.pallas_call(
        functools.partial(kernel, n),
        out_shape=pltpu.VMEM((kdim * per, size), f32),
        in_specs=[hbm, hbm, hbm, hbm],
        out_specs=pl.BlockSpec(memory_space=pltpu.VMEM),
        scratch_shapes=[
            pltpu.VMEM((2, padded * ydev, wide), f32),
            pltpu.VMEM((n1, size), f32),
            pltpu.VMEM((n2, size), f32),
            pltpu.SMEM((2,), jnp.int32),
            pltpu.VMEM((2, size, wide), f32),
            pltpu.VMEM((size, wide), f32),
            pltpu.VMEM((size, wide), f32),
            pltpu.VMEM((chips - 1, rows, wide), f32),
            pltpu.VMEM((2, size, wide), f32),
            pltpu.VMEM((padded, ydev, size), f32),
            pltpu.VMEM((KB, n2, size), f32),
            pltpu.VMEM((size, 2 * size), f32),
            pltpu.VMEM((size, size), f32),
            pltpu.VMEM((KB * size, n2), f32),
            pltpu.VMEM((size, n2), f32),
            pltpu.VMEM((holders, rows, n2), f32),
            pltpu.VMEM((size, n2), f32),
            pltpu.VMEM((n, KB, per, size), f32),
            pltpu.VMEM((holders, KB, per, size), f32),
            pltpu.SemaphoreType.DMA((5,)),
            pltpu.SemaphoreType.DMA((9,)),
            pltpu.SemaphoreType.DMA((9,)),
        ],
        compiler_params=pltpu.CompilerParams(
            collective_id=0, has_side_effects=True, vmem_limit_bytes=56 * 1024 * 1024
        ),
        cost_estimate=pl.CostEstimate(
            flops=600_000_000, bytes_accessed=2_000_000, transcendentals=256
        ),
    )(lines, sketch_one, sketch_two, ranks)
    return jnp.transpose(core.reshape(kdim, per, size), (1, 0, 2))


def solution(mesh):
    n = mesh.shape["wide"]

    def per_device(field, sketch_one, sketch_two, ranks):
        ydev, kdim, n1 = field.shape
        n2, size = sketch_two.shape
        fits = (
            mesh.shape["narrow"] == 1
            and size == 128
            and n == 32
            and ydev == 8
            and kdim <= 2 * PLANE * KB - KB
            and kdim > 2 * PLANE * KB - 2 * KB
            and n1 == 512
            and n2 == 8 * n
        )
        if fits:
            return fused(n, field, sketch_one, sketch_two, ranks)
        return general(field, sketch_one, sketch_two, ranks)

    return jax.shard_map(
        per_device,
        mesh=mesh,
        in_specs=(P("wide", "narrow", None), P(), P(), P()),
        out_specs=P("wide", "narrow", None),
        check_vma=False,
    )
```

```python
import functools

import jax
import jax.numpy as jnp
from jax import lax
from jax.experimental import pallas as pl
from jax.experimental.pallas import tpu as pltpu
from jax.sharding import PartitionSpec as P

HIGHEST = lax.Precision.HIGHEST
MESH = pl.DeviceIdType.MESH


def make_basis(local, sketch, rank):
    keep = (jnp.arange(sketch.shape[1]) < rank).astype(jnp.float32)
    masked = sketch * keep
    part = jnp.einsum("akn,ns->aks", local, masked, precision=HIGHEST)
    part = jnp.einsum("akn,aks->ns", local, part, precision=HIGHEST)
    sketched = lax.psum(part, ("wide", "narrow"))
    inner = jnp.dot(sketched.T, sketched, precision=HIGHEST) + jnp.diag(1.0 - keep)
    lower = jnp.linalg.cholesky(inner)
    return jax.scipy.linalg.solve_triangular(lower, sketched.T, lower=True)


def general(field, sketch_one, sketch_two, ranks):
    basis_one = make_basis(field, sketch_one, ranks[0])
    core_one = jnp.einsum("rn,ykn->rky", basis_one, field, precision=HIGHEST)
    regrouped = lax.all_to_all(core_one, "wide", split_axis=0, concat_axis=2, tiled=True)
    basis_two = make_basis(regrouped, sketch_two, ranks[1])
    return jnp.einsum("sn,rkn->rks", basis_two, regrouped, precision=HIGHEST)


def dot(a, b, dims):
    return lax.dot_general(
        a, b, (dims, ((), ())), precision=HIGHEST, preferred_element_type=jnp.float32
    )


def halves(x):
    high = x.astype(jnp.bfloat16)
    return high, (x - high.astype(jnp.float32)).astype(jnp.bfloat16)


def mul(a, b, dims):
    def one(x, y):
        return lax.dot_general(
            x, y, (dims, ((), ())), preferred_element_type=jnp.float32
        )

    (ah, al), (bh, bl) = halves(a), halves(b)
    return one(ah, bh) + (one(ah, bl) + one(al, bh))


NN = ((1,), (0,))
NT = ((1,), (1,))
TN = ((0,), (0,))
BLOCK = 8
TILES = 8
KB = 3
PLANE = 8


def inverse_factor(work, linv):
    size = linv.shape[0]
    tile = (BLOCK, size)
    group = TILES * BLOCK
    sub = lax.broadcasted_iota(jnp.int32, tile, 0)

    for r0 in range(0, size, group):
        own = work[r0 : r0 + group, :size]
        rest = work[r0 : r0 + group, size:]
        rows_a = [own[u * BLOCK : (u + 1) * BLOCK, :] for u in range(TILES)]
        rows_t = [rest[u * BLOCK : (u + 1) * BLOCK, :] for u in range(TILES)]
        panels_a, panels_t = [], []
        ahead = None
        for u in range(TILES):
            d, below = {}, {}
            for q in range(BLOCK):
                lane = r0 + u * BLOCK + q
                if ahead is None:
                    column = jnp.broadcast_to(rows_a[u][:, lane : lane + 1], tile)
                else:
                    column = ahead[q]
                for p in range(q, BLOCK):
                    d[p, q] = jnp.broadcast_to(column[p : p + 1, :], tile)
                for v in range(u + 1, TILES):
                    below[v, q] = jnp.broadcast_to(rows_a[v][:, lane : lane + 1], tile)
            ahead = None
            if u + 1 < TILES:
                first = r0 + (u + 1) * BLOCK
                ahead = [
                    jnp.broadcast_to(rows_a[u + 1][:, first + q : first + q + 1], tile)
                    for q in range(BLOCK)
                ]
            m = {}
            done_a, done_t = [], []
            panel_a = jnp.zeros(tile, jnp.float32)
            panel_t = jnp.zeros(tile, jnp.float32)
            for j in range(BLOCK):
                x = d[j, j]
                r = 1.0 / x
                y = lax.rsqrt(x)
                for q in range(j + 1, BLOCK):
                    for p in range(q, BLOCK):
                        d[p, q] = d[p, q] - (d[p, j] * d[q, j]) * r
                for p in range(j + 1, BLOCK):
                    m[p, j] = d[p, j] * r
                low = {}
                for v in range(u + 1, TILES):
                    low[v] = below[v, j] * r
                    if v == u + 1:
                        for q in range(BLOCK):
                            across = jnp.broadcast_to(below[v, j][q : q + 1, :], tile)
                            ahead[q] = ahead[q] - low[v] * across
                    for q in range(j + 1, BLOCK):
                        below[v, q] = below[v, q] - low[v] * d[q, j]
                ra = jnp.broadcast_to(rows_a[u][j : j + 1, :], tile)
                rt = jnp.broadcast_to(rows_t[u][j : j + 1, :], tile)
                for k in range(j):
                    ra = ra - m[j, k] * done_a[k]
                    rt = rt - m[j, k] * done_t[k]
                done_a.append(ra)
                done_t.append(rt)
                panel_a = jnp.where(sub == j, ra * y, panel_a)
                panel_t = jnp.where(sub == j, rt * y, panel_t)
                for v in range(u + 1, TILES):
                    rows_a[v] = rows_a[v] - low[v] * ra
                    rows_t[v] = rows_t[v] - low[v] * rt
            panels_a.append(panel_a)
            panels_t.append(panel_t)
        panel_t = jnp.concatenate(panels_t, axis=0)
        panel_a = jnp.concatenate(panels_a, axis=0)
        linv[r0 : r0 + group, :] = panel_t
        end = r0 + group
        if end < size:
            both = jnp.concatenate([panel_a, panel_t], axis=1)
            work[end:, :] = work[end:, :] - dot(panel_a.T[end:, :], both, NN)


def fill_work(work, inner, keep_row, size):
    row = lax.broadcasted_iota(jnp.int32, (size, size), 0)
    col = lax.broadcasted_iota(jnp.int32, (size, size), 1)
    eye = (row == col).astype(jnp.float32)
    work[:, :size] = inner + eye * (1.0 - keep_row)
    work[:, size:] = eye


def far_first(bits, low):
    def hops(m):
        flat = sum((m >> b) & 1 for b in range(low))
        return flat + (m >> low)

    return sorted(range(1, 1 << bits), key=lambda m: -hops(m))


def kernel(
    n, field, sketch_one, sketch_two, ranks_in, out,
    flat, s1, s2, ranks, part, pair, mine, got, full, rot, have, work, linv, stack,
    part_two, got_two, full_two, give, last,
    load_sem, send_sem, recv_sem, note,
):
    me = lax.axis_index("wide")
    size = s1.shape[1]
    wide = flat.shape[2]
    holders = last.shape[0]
    lines = field.shape[0]
    ydev = rot.shape[1]
    n2 = s2.shape[0]
    per = size // n
    chips = n // 2
    rows = size // chips
    core = lax.rem(me, 2)
    chip = me // 2

    loads = [
        pltpu.make_async_copy(ranks_in, ranks, load_sem.at[0]),
        pltpu.make_async_copy(sketch_one, s1, load_sem.at[1]),
    ] + [
        pltpu.make_async_copy(
            field.at[:, pl.ds(wide * h, wide)],
            flat.at[h, pl.ds(0, lines), :],
            load_sem.at[2 + h],
        )
        for h in range(2)
    ] + [
        pltpu.make_async_copy(sketch_two, s2, load_sem.at[4]),
    ]
    for load in loads:
        load.start()

    barrier = pltpu.get_barrier_semaphore()

    def greet(i, carry):
        peer = 2 * lax.rem(chip + 1 + i, chips) + 1
        pl.semaphore_signal(barrier, inc=1, device_id={"wide": peer}, device_id_type=MESH)
        return carry

    lax.fori_loop(0, chips - 1, greet, 0)
    leads = core == 1
    follows = core == 0
    twin = chip * 2 + 1 - core

    def nod():
        pl.semaphore_signal(note, inc=1, device_id={"wide": twin}, device_id_type=MESH)

    @pl.when(leads)
    def _():
        pl.semaphore_signal(barrier, inc=1, device_id={"wide": twin}, device_id_type=MESH)

    @pl.when(follows)
    def _():
        pl.semaphore_wait(barrier, 1)
        nod()

    bits = n.bit_length() - 1
    deltas = [(1 - 2 * lax.rem(me // (1 << b), 2)) * (1 << b) for b in range(bits)]

    def flipped(m):
        return me + sum(deltas[b] for b in range(bits) if (m >> b) & 1)

    alike = [(2 * m, flipped(2 * m)) for m in far_first(bits - 1, 2)]

    def copy(phase, source, target, peer):
        return pltpu.make_async_remote_copy(
            src_ref=source, dst_ref=target,
            send_sem=send_sem.at[phase], recv_sem=recv_sem.at[phase],
            device_id={"wide": peer}, device_id_type=MESH,
        )

    waits = []

    def later(phase, sent, when=None):
        def wait():
            copy(phase, sent, sent, twin).wait_send()

        waits.append(wait if when is None else functools.partial(pl.when(when), wait))

    def of_chip(c):
        return pl.ds(pl.multiple_of(c * rows, rows), rows)

    plane = me // PLANE
    below = me - plane * PLANE
    middle = jnp.logical_or(plane == 1, plane == 2)
    outside = jnp.logical_not(middle)
    slot = jnp.clip(me - PLANE, 0, 2 * PLANE - 1)
    holds = jnp.logical_and(middle, slot < holders)
    spare = jnp.logical_not(holds)
    turns = (6, 7, 4, 5, 2, 3, 1, 0)
    inside = [below + sum(deltas[b] for b in range(3) if (m >> b) & 1) for m in turns]
    nearer = jnp.where(plane < 2, PLANE, 2 * PLANE)
    farther = 3 * PLANE - nearer
    group = [b + farther for b in inside] + [b + nearer for b in inside[:-1]]
    edges = [b + 3 * (farther - PLANE) for b in inside] + [
        b + 3 * (nearer - PLANE) for b in inside
    ]

    for h in range(2):
        flat[h, lines:, :] = jnp.zeros((flat.shape[1] - lines, wide), jnp.float32)
    loads[0].wait()
    lane = lax.broadcasted_iota(jnp.int32, (1, size), 1)
    sub = lax.broadcasted_iota(jnp.int32, (size, 1), 0)
    keep_one = (lane < ranks[0]).astype(jnp.float32)
    keep_two = (lane < ranks[1]).astype(jnp.float32)
    loads[1].wait()
    turned = s1[...].T * (sub < ranks[0]).astype(jnp.float32)
    loads[2].wait()
    projected = mul(turned[:, :wide], flat[0, :lines, :], NT)
    loads[3].wait()
    projected = projected + mul(turned[:, wide:], flat[1, :lines, :], NT)
    part[1 - core] = mul(projected, flat[1 - core, pl.ds(0, lines), :], NN)

    @pl.when(leads)
    def _():
        pl.semaphore_wait(note, 1)

    copy(0, part.at[1 - core], pair, twin).start()
    later(0, pair)
    part[core] = mul(projected, flat[core, pl.ds(0, lines), :], NN)
    copy(0, pair, pair, twin).wait_recv()
    mine[...] = part[core] + pair[...]

    @pl.when(leads)
    def _():
        pl.semaphore_wait(barrier, n - 2)
        nod()

    @pl.when(follows)
    def _():
        pl.semaphore_wait(note, 1)

    for i, (m, peer) in enumerate(alike):
        copy(1, mine.at[of_chip(peer // 2), :], got.at[m // 2 - 1], peer).start()
    later(1, got)
    loads[4].wait()
    masked_two = (s2[...].T) * (sub < ranks[1]).astype(jnp.float32)
    s2t = masked_two
    copy(1, got, got, twin).wait_recv()
    full[core, of_chip(chip), :] = jnp.sum(got[...], axis=0) + mine[of_chip(chip), :]
    for m, peer in alike:
        own = full.at[core, of_chip(chip), :]
        copy(2, own, own, peer).start()
    later(2, got)
    copy(2, got, got, twin).wait_recv()
    copy(3, full.at[core], full.at[core], twin).start()
    later(3, pair)
    sk = full[core]
    rot[...] = mul(flat[core], sk, NT).reshape(rot.shape)
    inner = dot(sk, sk, NT)
    copy(3, pair, pair, twin).wait_recv()
    sk = full[1 - core]

    mine_y = pl.ds(pl.multiple_of(me * ydev, ydev), ydev)
    part_lines = PLANE * KB * ydev
    for base in (farther, nearer):
        first = base - PLANE
        ks = pl.ds(KB * first, KB * PLANE)
        span = pl.ds(pl.multiple_of(first * (KB * ydev), part_lines), part_lines)
        more = mul(flat[1 - core, span, :], sk, NT)
        rot[ks] = rot[ks] + more.reshape(KB * PLANE, ydev, size)
        for b in inside:
            peer = b + base
            j = peer - PLANE

            @pl.when(jnp.logical_and(j < holders, peer != me))
            def _():
                copy(
                    4, rot.at[pl.ds(KB * j, KB)], have.at[:, mine_y, :], peer
                ).start()

    later(4, rot.at[pl.ds(0, KB * (holders - 1))], holds)
    later(4, rot.at[pl.ds(0, KB * holders)], spare)

    @pl.when(holds)
    def _():
        have[:, mine_y, :] = rot[pl.ds(KB * slot, KB)]

    inner = inner + dot(sk, sk, NT)
    fill_work(work, inner, keep_one, size)
    inverse_factor(work, linv)

    @pl.when(holds)
    def _():
        everything = have.at[:, pl.ds(0, n2 - ydev), :]
        copy(4, everything, everything, twin).wait_recv()

    @pl.when(holds)
    def _():
        for k in range(KB):
            stack[k * size : (k + 1) * size, :] = mul(linv[...], have[k], NT)
        mixed = stack[...]
        spread = mul(s2t, mixed, NT)
        total = mul(spread, mixed, NN)
        part_two[...] = total

    def of_slot(j):
        place = lax.rem(j, 2) * PLANE + j // 2
        return pl.ds(pl.multiple_of(place * rows, rows), rows)

    @pl.when(holds)
    def _():
        for peer in group:
            copy(6, part_two.at[of_slot(peer - PLANE), :], got_two.at[slot], peer).start()
        got_two[slot] = part_two[of_slot(slot), :]
        most = got_two.at[pl.ds(0, holders - 1)]
        copy(6, most, most, twin).wait_recv()

    @pl.when(jnp.logical_and(middle, spare))
    def _():
        copy(6, got_two, got_two, twin).wait_recv()

    later(6, part_two.at[pl.ds(0, size - rows), :], holds)
    most_two = full_two.at[pl.ds(0, size - rows), :]

    @pl.when(middle)
    def _():
        own = full_two.at[of_slot(slot), :]
        own[...] = jnp.sum(got_two[...], axis=0)
        for peer in group:
            copy(7, own, own, peer).start()
        for peer in edges:
            copy(5, own, own, peer).start()
        copy(7, most_two, most_two, twin).wait_recv()

    @pl.when(outside)
    def _():
        copy(5, full_two, full_two, twin).wait_recv()

    later(7, most_two, middle)
    later(5, full_two, middle)

    @pl.when(holds)
    def _():
        spun = mul(stack[...], full_two[...], NT)
        for d in range(n):
            for k in range(KB):
                give[d, k] = spun[k * size + per * d : k * size + per * (d + 1), :]
        for peer in edges + group:
            copy(8, give.at[peer], last.at[slot], peer).start()
        last[slot] = give[me]

    later(8, give.at[pl.ds(0, n - 1)], holds)
    sk = full_two[...]
    fill_work(work, mul(sk, sk, NT), keep_two, size)
    inverse_factor(work, linv)

    @pl.when(holds)
    def _():
        most = last.at[pl.ds(0, holders - 1)]
        copy(8, most, most, twin).wait_recv()

    @pl.when(spare)
    def _():
        copy(8, last, last, twin).wait_recv()

    done = mul(last[...].reshape(holders * KB * per, size), linv[...], NT)
    out[...] = done[: out.shape[0], :]

    for wait in waits:
        wait()


def fused(n, field, sketch_one, sketch_two, ranks):
    ydev, kdim, n1 = field.shape
    n2, size = sketch_two.shape
    chips = n // 2
    rows = size // chips
    wide = n1 // 2
    holders = -(-kdim // KB)
    padded = 2 * PLANE * KB
    per = size // n
    hbm = pl.BlockSpec(memory_space=pltpu.MemorySpace.HBM)
    f32 = jnp.float32
    lines = jnp.transpose(field, (1, 0, 2)).reshape(kdim * ydev, n1)
    core = pl.pallas_call(
        functools.partial(kernel, n),
        out_shape=pltpu.VMEM((kdim * per, size), f32),
        in_specs=[hbm, hbm, hbm, hbm],
        out_specs=pl.BlockSpec(memory_space=pltpu.VMEM),
        scratch_shapes=[
            pltpu.VMEM((2, padded * ydev, wide), f32),
            pltpu.VMEM((n1, size), f32),
            pltpu.VMEM((n2, size), f32),
            pltpu.SMEM((2,), jnp.int32),
            pltpu.VMEM((2, size, wide), f32),
            pltpu.VMEM((size, wide), f32),
            pltpu.VMEM((size, wide), f32),
            pltpu.VMEM((chips - 1, rows, wide), f32),
            pltpu.VMEM((2, size, wide), f32),
            pltpu.VMEM((padded, ydev, size), f32),
            pltpu.VMEM((KB, n2, size), f32),
            pltpu.VMEM((size, 2 * size), f32),
            pltpu.VMEM((size, size), f32),
            pltpu.VMEM((KB * size, n2), f32),
            pltpu.VMEM((size, n2), f32),
            pltpu.VMEM((holders, rows, n2), f32),
            pltpu.VMEM((size, n2), f32),
            pltpu.VMEM((n, KB, per, size), f32),
            pltpu.VMEM((holders, KB, per, size), f32),
            pltpu.SemaphoreType.DMA((5,)),
            pltpu.SemaphoreType.DMA((9,)),
            pltpu.SemaphoreType.DMA((9,)),
            pltpu.SemaphoreType.REGULAR,
        ],
        compiler_params=pltpu.CompilerParams(
            collective_id=0, has_side_effects=True, vmem_limit_bytes=56 * 1024 * 1024
        ),
        cost_estimate=pl.CostEstimate(
            flops=600_000_000, bytes_accessed=2_000_000, transcendentals=256
        ),
    )(lines, sketch_one, sketch_two, ranks)
    return jnp.transpose(core.reshape(kdim, per, size), (1, 0, 2))


def solution(mesh):
    n = mesh.shape["wide"]

    def per_device(field, sketch_one, sketch_two, ranks):
        ydev, kdim, n1 = field.shape
        n2, size = sketch_two.shape
        fits = (
            mesh.shape["narrow"] == 1
            and size == 128
            and n == 32
            and ydev == 8
            and kdim <= 2 * PLANE * KB - KB
            and kdim > 2 * PLANE * KB - 2 * KB
            and n1 == 512
            and n2 == 8 * n
        )
        if fits:
            return fused(n, field, sketch_one, sketch_two, ranks)
        return general(field, sketch_one, sketch_two, ranks)

    return jax.shard_map(
        per_device,
        mesh=mesh,
        in_specs=(P("wide", "narrow", None), P(), P(), P()),
        out_specs=P("wide", "narrow", None),
        check_vma=False,
    )
```

```python
import functools

import jax
import jax.numpy as jnp
from jax import lax
from jax.experimental import pallas as pl
from jax.experimental.pallas import tpu as pltpu
from jax.sharding import PartitionSpec as P

HIGHEST = lax.Precision.HIGHEST
MESH = pl.DeviceIdType.MESH


def make_basis(local, sketch, rank):
    keep = (jnp.arange(sketch.shape[1]) < rank).astype(jnp.float32)
    masked = sketch * keep
    part = jnp.einsum("akn,ns->aks", local, masked, precision=HIGHEST)
    part = jnp.einsum("akn,aks->ns", local, part, precision=HIGHEST)
    sketched = lax.psum(part, ("wide", "narrow"))
    inner = jnp.dot(sketched.T, sketched, precision=HIGHEST) + jnp.diag(1.0 - keep)
    lower = jnp.linalg.cholesky(inner)
    return jax.scipy.linalg.solve_triangular(lower, sketched.T, lower=True)


def general(field, sketch_one, sketch_two, ranks):
    basis_one = make_basis(field, sketch_one, ranks[0])
    core_one = jnp.einsum("rn,ykn->rky", basis_one, field, precision=HIGHEST)
    regrouped = lax.all_to_all(core_one, "wide", split_axis=0, concat_axis=2, tiled=True)
    basis_two = make_basis(regrouped, sketch_two, ranks[1])
    return jnp.einsum("sn,rkn->rks", basis_two, regrouped, precision=HIGHEST)


def dot(a, b, dims):
    return lax.dot_general(
        a, b, (dims, ((), ())), precision=HIGHEST, preferred_element_type=jnp.float32
    )


def halves(x):
    high = x.astype(jnp.bfloat16)
    return high, (x - high.astype(jnp.float32)).astype(jnp.bfloat16)


def mul(a, b, dims):
    def one(x, y):
        return lax.dot_general(
            x, y, (dims, ((), ())), preferred_element_type=jnp.float32
        )

    (ah, al), (bh, bl) = halves(a), halves(b)
    rest = one(al, bh)
    if dims == NT and b.shape[1] == 128:
        joined = one(
            jnp.concatenate([ah, ah], axis=1), jnp.concatenate([bh, bl], axis=1)
        )
        return joined + rest
    if dims == NT and b.shape[0] == 128:
        joined = one(ah, jnp.concatenate([bh, bl], axis=0))
        return joined[:, :128] + (joined[:, 128:] + rest)
    return one(ah, bh) + (one(ah, bl) + rest)


NN = ((1,), (0,))
NT = ((1,), (1,))
TN = ((0,), (0,))
BLOCK = 8
TILES = 8
KB = 3
PLANE = 8


def inverse_factor(work, linv):
    size = linv.shape[0]
    tile = (BLOCK, size)
    group = TILES * BLOCK
    sub = lax.broadcasted_iota(jnp.int32, tile, 0)

    for r0 in range(0, size, group):
        own = work[r0 : r0 + group, :size]
        rest = work[r0 : r0 + group, size:]
        rows_a = [own[u * BLOCK : (u + 1) * BLOCK, :] for u in range(TILES)]
        rows_t = [rest[u * BLOCK : (u + 1) * BLOCK, :] for u in range(TILES)]
        panels_a, panels_t = [], []
        ahead = None
        for u in range(TILES):
            d, below = {}, {}
            for q in range(BLOCK):
                lane = r0 + u * BLOCK + q
                if ahead is None:
                    column = jnp.broadcast_to(rows_a[u][:, lane : lane + 1], tile)
                else:
                    column = ahead[q]
                for p in range(q, BLOCK):
                    d[p, q] = jnp.broadcast_to(column[p : p + 1, :], tile)
                for v in range(u + 1, TILES):
                    below[v, q] = jnp.broadcast_to(rows_a[v][:, lane : lane + 1], tile)
            ahead = None
            if u + 1 < TILES:
                first = r0 + (u + 1) * BLOCK
                ahead = [
                    jnp.broadcast_to(rows_a[u + 1][:, first + q : first + q + 1], tile)
                    for q in range(BLOCK)
                ]
            m = {}
            done_a, done_t = [], []
            panel_a = jnp.zeros(tile, jnp.float32)
            panel_t = jnp.zeros(tile, jnp.float32)
            for j in range(BLOCK):
                x = d[j, j]
                r = 1.0 / x
                y = lax.rsqrt(x)
                for q in range(j + 1, BLOCK):
                    for p in range(q, BLOCK):
                        d[p, q] = d[p, q] - (d[p, j] * d[q, j]) * r
                for p in range(j + 1, BLOCK):
                    m[p, j] = d[p, j] * r
                low = {}
                for v in range(u + 1, TILES):
                    low[v] = below[v, j] * r
                    if v == u + 1:
                        for q in range(BLOCK):
                            across = jnp.broadcast_to(below[v, j][q : q + 1, :], tile)
                            ahead[q] = ahead[q] - low[v] * across
                    for q in range(j + 1, BLOCK):
                        below[v, q] = below[v, q] - low[v] * d[q, j]
                ra = jnp.broadcast_to(rows_a[u][j : j + 1, :], tile)
                rt = jnp.broadcast_to(rows_t[u][j : j + 1, :], tile)
                for k in range(j):
                    ra = ra - m[j, k] * done_a[k]
                    rt = rt - m[j, k] * done_t[k]
                done_a.append(ra)
                done_t.append(rt)
                panel_a = jnp.where(sub == j, ra * y, panel_a)
                panel_t = jnp.where(sub == j, rt * y, panel_t)
                for v in range(u + 1, TILES):
                    rows_a[v] = rows_a[v] - low[v] * ra
                    rows_t[v] = rows_t[v] - low[v] * rt
            panels_a.append(panel_a)
            panels_t.append(panel_t)
        panel_t = jnp.concatenate(panels_t, axis=0)
        panel_a = jnp.concatenate(panels_a, axis=0)
        linv[r0 : r0 + group, :] = panel_t
        end = r0 + group
        if end < size:
            both = jnp.concatenate([panel_a, panel_t], axis=1)
            work[end:, :] = work[end:, :] - dot(panel_a.T[end:, :], both, NN)


def fill_work(work, inner, keep_row, size):
    row = lax.broadcasted_iota(jnp.int32, (size, size), 0)
    col = lax.broadcasted_iota(jnp.int32, (size, size), 1)
    eye = (row == col).astype(jnp.float32)
    work[:, :size] = inner + eye * (1.0 - keep_row)
    work[:, size:] = eye


def far_first(bits, low):
    def hops(m):
        flat = sum((m >> b) & 1 for b in range(low))
        return flat + (m >> low)

    return sorted(range(1, 1 << bits), key=lambda m: -hops(m))


def kernel(
    n, field, sketch_one, sketch_two, ranks_in, out,
    flat, s1, s2, ranks, part, pair, mine, got, full, rot, have, work, linv, stack,
    part_two, got_two, full_two, give, last,
    load_sem, send_sem, recv_sem, note,
):
    me = lax.axis_index("wide")
    size = s1.shape[1]
    wide = flat.shape[2]
    holders = last.shape[0]
    lines = field.shape[0]
    ydev = rot.shape[1]
    n2 = s2.shape[0]
    per = size // n
    chips = n // 2
    rows = size // chips
    core = lax.rem(me, 2)
    chip = me // 2

    loads = [
        pltpu.make_async_copy(ranks_in, ranks, load_sem.at[0]),
        pltpu.make_async_copy(sketch_one, s1, load_sem.at[1]),
    ] + [
        pltpu.make_async_copy(
            field.at[:, pl.ds(wide * h, wide)],
            flat.at[h, pl.ds(0, lines), :],
            load_sem.at[2 + h],
        )
        for h in range(2)
    ] + [
        pltpu.make_async_copy(sketch_two, s2, load_sem.at[4]),
    ]
    for load in loads:
        load.start()

    barrier = pltpu.get_barrier_semaphore()

    def greet(i, carry):
        peer = 2 * lax.rem(chip + 1 + i, chips) + 1
        pl.semaphore_signal(barrier, inc=1, device_id={"wide": peer}, device_id_type=MESH)
        return carry

    lax.fori_loop(0, chips - 1, greet, 0)
    leads = core == 1
    follows = core == 0
    twin = chip * 2 + 1 - core

    def nod():
        pl.semaphore_signal(note, inc=1, device_id={"wide": twin}, device_id_type=MESH)

    @pl.when(leads)
    def _():
        pl.semaphore_signal(barrier, inc=1, device_id={"wide": twin}, device_id_type=MESH)

    @pl.when(follows)
    def _():
        pl.semaphore_wait(barrier, 1)
        nod()

    bits = n.bit_length() - 1
    deltas = [(1 - 2 * lax.rem(me // (1 << b), 2)) * (1 << b) for b in range(bits)]

    def flipped(m):
        return me + sum(deltas[b] for b in range(bits) if (m >> b) & 1)

    alike = [(2 * m, flipped(2 * m)) for m in far_first(bits - 1, 2)]

    def copy(phase, source, target, peer):
        return pltpu.make_async_remote_copy(
            src_ref=source, dst_ref=target,
            send_sem=send_sem.at[phase], recv_sem=recv_sem.at[phase],
            device_id={"wide": peer}, device_id_type=MESH,
        )

    waits = []

    def later(phase, sent, when=None):
        def wait():
            copy(phase, sent, sent, twin).wait_send()

        waits.append(wait if when is None else functools.partial(pl.when(when), wait))

    def of_chip(c):
        return pl.ds(pl.multiple_of(c * rows, rows), rows)

    plane = me // PLANE
    below = me - plane * PLANE
    middle = jnp.logical_or(plane == 1, plane == 2)
    outside = jnp.logical_not(middle)
    slot = jnp.clip(me - PLANE, 0, 2 * PLANE - 1)
    holds = jnp.logical_and(middle, slot < holders)
    spare = jnp.logical_not(holds)
    turns = (7, 6, 5, 4, 3, 2, 1, 0)
    inside = [below + sum(deltas[b] for b in range(3) if (m >> b) & 1) for m in turns]
    nearer = jnp.where(plane < 2, PLANE, 2 * PLANE)
    farther = 3 * PLANE - nearer
    group = [b + farther for b in inside] + [b + nearer for b in inside[:-1]]
    edges = [b + 3 * (farther - PLANE) for b in inside] + [
        b + 3 * (nearer - PLANE) for b in inside
    ]

    for h in range(2):
        flat[h, lines:, :] = jnp.zeros((flat.shape[1] - lines, wide), jnp.float32)
    loads[0].wait()
    lane = lax.broadcasted_iota(jnp.int32, (1, size), 1)
    sub = lax.broadcasted_iota(jnp.int32, (size, 1), 0)
    keep_one = (lane < ranks[0]).astype(jnp.float32)
    keep_two = (lane < ranks[1]).astype(jnp.float32)
    loads[1].wait()
    turned = s1[...].T * (sub < ranks[0]).astype(jnp.float32)
    loads[2].wait()
    projected = mul(turned[:, :wide], flat[0, :lines, :], NT)
    loads[3].wait()
    projected = projected + mul(turned[:, wide:], flat[1, :lines, :], NT)
    part[1 - core] = mul(projected, flat[1 - core, pl.ds(0, lines), :], NN)

    @pl.when(leads)
    def _():
        pl.semaphore_wait(note, 1)

    copy(0, part.at[1 - core], pair, twin).start()
    later(0, pair)
    part[core] = mul(projected, flat[core, pl.ds(0, lines), :], NN)
    copy(0, pair, pair, twin).wait_recv()
    mine[...] = part[core] + pair[...]

    @pl.when(leads)
    def _():
        pl.semaphore_wait(barrier, n - 2)
        nod()

    @pl.when(follows)
    def _():
        pl.semaphore_wait(note, 1)

    for i, (m, peer) in enumerate(alike):
        copy(1, mine.at[of_chip(peer // 2), :], got.at[m // 2 - 1], peer).start()
    later(1, got)
    loads[4].wait()
    masked_two = (s2[...].T) * (sub < ranks[1]).astype(jnp.float32)
    s2t = masked_two
    copy(1, got, got, twin).wait_recv()
    full[core, of_chip(chip), :] = jnp.sum(got[...], axis=0) + mine[of_chip(chip), :]
    for m, peer in alike:
        own = full.at[core, of_chip(chip), :]
        copy(2, own, own, peer).start()
    later(2, got)
    copy(2, got, got, twin).wait_recv()
    copy(3, full.at[core], full.at[core], twin).start()
    later(3, pair)
    sk = full[core]
    rot[...] = mul(flat[core], sk, NT).reshape(rot.shape)
    inner = mul(sk, sk, NT)
    copy(3, pair, pair, twin).wait_recv()
    sk = full[1 - core]

    mine_y = pl.ds(pl.multiple_of(me * ydev, ydev), ydev)
    part_lines = PLANE * KB * ydev
    for base in (farther, nearer):
        first = base - PLANE
        ks = pl.ds(KB * first, KB * PLANE)
        span = pl.ds(pl.multiple_of(first * (KB * ydev), part_lines), part_lines)
        more = mul(flat[1 - core, span, :], sk, NT)
        rot[ks] = rot[ks] + more.reshape(KB * PLANE, ydev, size)
        for b in inside:
            peer = b + base
            j = peer - PLANE

            @pl.when(jnp.logical_and(j < holders, peer != me))
            def _():
                copy(
                    4, rot.at[pl.ds(KB * j, KB)], have.at[:, mine_y, :], peer
                ).start()

    later(4, rot.at[pl.ds(0, KB * (holders - 1))], holds)
    later(4, rot.at[pl.ds(0, KB * holders)], spare)

    @pl.when(holds)
    def _():
        have[:, mine_y, :] = rot[pl.ds(KB * slot, KB)]

    inner = inner + mul(sk, sk, NT)
    fill_work(work, inner, keep_one, size)
    inverse_factor(work, linv)

    @pl.when(holds)
    def _():
        everything = have.at[:, pl.ds(0, n2 - ydev), :]
        copy(4, everything, everything, twin).wait_recv()

    @pl.when(holds)
    def _():
        for k in range(KB):
            stack[k * size : (k + 1) * size, :] = mul(linv[...], have[k], NT)
        mixed = stack[...]
        spread = mul(s2t, mixed, NT)
        total = mul(spread, mixed, NN)
        part_two[...] = total

    def of_slot(j):
        place = lax.rem(j, 2) * PLANE + j // 2
        return pl.ds(pl.multiple_of(place * rows, rows), rows)

    @pl.when(holds)
    def _():
        for peer in group:
            copy(6, part_two.at[of_slot(peer - PLANE), :], got_two.at[slot], peer).start()
        got_two[slot] = part_two[of_slot(slot), :]
        most = got_two.at[pl.ds(0, holders - 1)]
        copy(6, most, most, twin).wait_recv()

    @pl.when(jnp.logical_and(middle, spare))
    def _():
        copy(6, got_two, got_two, twin).wait_recv()

    later(6, part_two.at[pl.ds(0, size - rows), :], holds)
    most_two = full_two.at[pl.ds(0, size - rows), :]

    @pl.when(middle)
    def _():
        own = full_two.at[of_slot(slot), :]
        own[...] = jnp.sum(got_two[...], axis=0)
        for peer in group:
            copy(7, own, own, peer).start()
        for peer in edges:
            copy(5, own, own, peer).start()
        copy(7, most_two, most_two, twin).wait_recv()

    @pl.when(outside)
    def _():
        copy(5, full_two, full_two, twin).wait_recv()

    later(7, most_two, middle)
    later(5, full_two, middle)

    @pl.when(holds)
    def _():
        spun = mul(stack[...], full_two[...], NT)
        for d in range(n):
            for k in range(KB):
                give[d, k] = spun[k * size + per * d : k * size + per * (d + 1), :]
        for peer in edges + group:
            copy(8, give.at[peer], last.at[slot], peer).start()
        last[slot] = give[me]

    later(8, give.at[pl.ds(0, n - 1)], holds)
    sk = full_two[...]
    fill_work(work, mul(sk, sk, NT), keep_two, size)
    inverse_factor(work, linv)

    @pl.when(holds)
    def _():
        most = last.at[pl.ds(0, holders - 1)]
        copy(8, most, most, twin).wait_recv()

    @pl.when(spare)
    def _():
        copy(8, last, last, twin).wait_recv()

    done = mul(last[...].reshape(holders * KB * per, size), linv[...], NT)
    out[...] = done[: out.shape[0], :]

    for wait in waits:
        wait()


def fused(n, field, sketch_one, sketch_two, ranks):
    ydev, kdim, n1 = field.shape
    n2, size = sketch_two.shape
    chips = n // 2
    rows = size // chips
    wide = n1 // 2
    holders = -(-kdim // KB)
    padded = 2 * PLANE * KB
    per = size // n
    hbm = pl.BlockSpec(memory_space=pltpu.MemorySpace.HBM)
    f32 = jnp.float32
    lines = jnp.transpose(field, (1, 0, 2)).reshape(kdim * ydev, n1)
    core = pl.pallas_call(
        functools.partial(kernel, n),
        out_shape=pltpu.VMEM((kdim * per, size), f32),
        in_specs=[hbm, hbm, hbm, hbm],
        out_specs=pl.BlockSpec(memory_space=pltpu.VMEM),
        scratch_shapes=[
            pltpu.VMEM((2, padded * ydev, wide), f32),
            pltpu.VMEM((n1, size), f32),
            pltpu.VMEM((n2, size), f32),
            pltpu.SMEM((2,), jnp.int32),
            pltpu.VMEM((2, size, wide), f32),
            pltpu.VMEM((size, wide), f32),
            pltpu.VMEM((size, wide), f32),
            pltpu.VMEM((chips - 1, rows, wide), f32),
            pltpu.VMEM((2, size, wide), f32),
            pltpu.VMEM((padded, ydev, size), f32),
            pltpu.VMEM((KB, n2, size), f32),
            pltpu.VMEM((size, 2 * size), f32),
            pltpu.VMEM((size, size), f32),
            pltpu.VMEM((KB * size, n2), f32),
            pltpu.VMEM((size, n2), f32),
            pltpu.VMEM((holders, rows, n2), f32),
            pltpu.VMEM((size, n2), f32),
            pltpu.VMEM((n, KB, per, size), f32),
            pltpu.VMEM((holders, KB, per, size), f32),
            pltpu.SemaphoreType.DMA((5,)),
            pltpu.SemaphoreType.DMA((9,)),
            pltpu.SemaphoreType.DMA((9,)),
            pltpu.SemaphoreType.REGULAR,
        ],
        compiler_params=pltpu.CompilerParams(
            collective_id=0, has_side_effects=True, vmem_limit_bytes=56 * 1024 * 1024
        ),
        cost_estimate=pl.CostEstimate(
            flops=600_000_000, bytes_accessed=2_000_000, transcendentals=256
        ),
    )(lines, sketch_one, sketch_two, ranks)
    return jnp.transpose(core.reshape(kdim, per, size), (1, 0, 2))


def solution(mesh):
    n = mesh.shape["wide"]

    def per_device(field, sketch_one, sketch_two, ranks):
        ydev, kdim, n1 = field.shape
        n2, size = sketch_two.shape
        fits = (
            mesh.shape["narrow"] == 1
            and size == 128
            and n == 32
            and ydev == 8
            and kdim <= 2 * PLANE * KB - KB
            and kdim > 2 * PLANE * KB - 2 * KB
            and n1 == 512
            and n2 == 8 * n
        )
        if fits:
            return fused(n, field, sketch_one, sketch_two, ranks)
        return general(field, sketch_one, sketch_two, ranks)

    return jax.shard_map(
        per_device,
        mesh=mesh,
        in_specs=(P("wide", "narrow", None), P(), P(), P()),
        out_specs=P("wide", "narrow", None),
        check_vma=False,
    )
```

```python
import functools

import jax
import jax.numpy as jnp
from jax import lax
from jax.experimental import pallas as pl
from jax.experimental.pallas import tpu as pltpu
from jax.sharding import PartitionSpec as P

HIGHEST = lax.Precision.HIGHEST
MESH = pl.DeviceIdType.MESH


def make_basis(local, sketch, rank):
    keep = (jnp.arange(sketch.shape[1]) < rank).astype(jnp.float32)
    masked = sketch * keep
    part = jnp.einsum("akn,ns->aks", local, masked, precision=HIGHEST)
    part = jnp.einsum("akn,aks->ns", local, part, precision=HIGHEST)
    sketched = lax.psum(part, ("wide", "narrow"))
    inner = jnp.dot(sketched.T, sketched, precision=HIGHEST) + jnp.diag(1.0 - keep)
    lower = jnp.linalg.cholesky(inner)
    return jax.scipy.linalg.solve_triangular(lower, sketched.T, lower=True)


def general(field, sketch_one, sketch_two, ranks):
    basis_one = make_basis(field, sketch_one, ranks[0])
    core_one = jnp.einsum("rn,ykn->rky", basis_one, field, precision=HIGHEST)
    regrouped = lax.all_to_all(core_one, "wide", split_axis=0, concat_axis=2, tiled=True)
    basis_two = make_basis(regrouped, sketch_two, ranks[1])
    return jnp.einsum("sn,rkn->rks", basis_two, regrouped, precision=HIGHEST)


def dot(a, b, dims):
    return lax.dot_general(
        a, b, (dims, ((), ())), precision=HIGHEST, preferred_element_type=jnp.float32
    )


def halves(x):
    high = x.astype(jnp.bfloat16)
    return high, (x - high.astype(jnp.float32)).astype(jnp.bfloat16)


def mul(a, b, dims):
    def one(x, y):
        return lax.dot_general(
            x, y, (dims, ((), ())), preferred_element_type=jnp.float32
        )

    (ah, al), (bh, bl) = halves(a), halves(b)
    rest = one(al, bh)
    if dims == NT and b.shape[1] == 128:
        joined = one(
            jnp.concatenate([ah, ah], axis=1), jnp.concatenate([bh, bl], axis=1)
        )
        return joined + rest
    if dims == NT and b.shape[0] == 128:
        joined = one(ah, jnp.concatenate([bh, bl], axis=0))
        return joined[:, :128] + (joined[:, 128:] + rest)
    return one(ah, bh) + (one(ah, bl) + rest)


NN = ((1,), (0,))
NT = ((1,), (1,))
TN = ((0,), (0,))
BLOCK = 8
TILES = 8
KB = 3
PLANE = 8


def inverse_factor(work, linv):
    size = linv.shape[0]
    tile = (BLOCK, size)
    group = TILES * BLOCK
    sub = lax.broadcasted_iota(jnp.int32, tile, 0)

    for r0 in range(0, size, group):
        own = work[r0 : r0 + group, :size]
        rest = work[r0 : r0 + group, size:]
        rows_a = [own[u * BLOCK : (u + 1) * BLOCK, :] for u in range(TILES)]
        rows_t = [rest[u * BLOCK : (u + 1) * BLOCK, :] for u in range(TILES)]
        panels_a, panels_t = [], []
        ahead = None
        for u in range(TILES):
            d, below = {}, {}
            for q in range(BLOCK):
                lane = r0 + u * BLOCK + q
                if ahead is None:
                    column = jnp.broadcast_to(rows_a[u][:, lane : lane + 1], tile)
                else:
                    column = ahead[q]
                for p in range(q, BLOCK):
                    d[p, q] = jnp.broadcast_to(column[p : p + 1, :], tile)
                for v in range(u + 1, TILES):
                    below[v, q] = jnp.broadcast_to(rows_a[v][:, lane : lane + 1], tile)
            ahead = None
            if u + 1 < TILES:
                first = r0 + (u + 1) * BLOCK
                ahead = [
                    jnp.broadcast_to(rows_a[u + 1][:, first + q : first + q + 1], tile)
                    for q in range(BLOCK)
                ]
            m = {}
            done_a, done_t = [], []
            panel_a = jnp.zeros(tile, jnp.float32)
            panel_t = jnp.zeros(tile, jnp.float32)
            for j in range(BLOCK):
                x = d[j, j]
                r = 1.0 / x
                y = lax.rsqrt(x)
                for q in range(j + 1, BLOCK):
                    for p in range(q, BLOCK):
                        d[p, q] = d[p, q] - (d[p, j] * d[q, j]) * r
                for p in range(j + 1, BLOCK):
                    m[p, j] = d[p, j] * r
                low = {}
                for v in range(u + 1, TILES):
                    low[v] = below[v, j] * r
                    if v == u + 1:
                        for q in range(BLOCK):
                            across = jnp.broadcast_to(below[v, j][q : q + 1, :], tile)
                            ahead[q] = ahead[q] - low[v] * across
                    for q in range(j + 1, BLOCK):
                        below[v, q] = below[v, q] - low[v] * d[q, j]
                ra = jnp.broadcast_to(rows_a[u][j : j + 1, :], tile)
                rt = jnp.broadcast_to(rows_t[u][j : j + 1, :], tile)
                for k in range(j):
                    ra = ra - m[j, k] * done_a[k]
                    rt = rt - m[j, k] * done_t[k]
                done_a.append(ra)
                done_t.append(rt)
                panel_a = jnp.where(sub == j, ra * y, panel_a)
                panel_t = jnp.where(sub == j, rt * y, panel_t)
                for v in range(u + 1, TILES):
                    rows_a[v] = rows_a[v] - low[v] * ra
                    rows_t[v] = rows_t[v] - low[v] * rt
            panels_a.append(panel_a)
            panels_t.append(panel_t)
        panel_t = jnp.concatenate(panels_t, axis=0)
        panel_a = jnp.concatenate(panels_a, axis=0)
        linv[r0 : r0 + group, :] = panel_t
        end = r0 + group
        if end < size:
            both = jnp.concatenate([panel_a, panel_t], axis=1)
            work[end:, :] = work[end:, :] - dot(panel_a.T[end:, :], both, NN)


def fill_work(work, inner, keep_row, size):
    row = lax.broadcasted_iota(jnp.int32, (size, size), 0)
    col = lax.broadcasted_iota(jnp.int32, (size, size), 1)
    eye = (row == col).astype(jnp.float32)
    work[:, :size] = inner + eye * (1.0 - keep_row)
    work[:, size:] = eye


def far_first(bits, low):
    def hops(m):
        flat = sum((m >> b) & 1 for b in range(low))
        return flat + (m >> low)

    return sorted(range(1, 1 << bits), key=lambda m: -hops(m))


def kernel(
    n, field, sketch_one, sketch_two, ranks_in, out,
    flat, s1, s2, ranks, part, pair, mine, got, full, rot, have, work, linv, stack,
    part_two, got_two, full_two, give, last,
    load_sem, send_sem, recv_sem, note,
):
    me = lax.axis_index("wide")
    size = s1.shape[1]
    wide = flat.shape[2]
    holders = last.shape[0]
    lines = field.shape[0]
    ydev = rot.shape[1]
    n2 = s2.shape[0]
    per = size // n
    chips = n // 2
    rows = size // chips
    core = lax.rem(me, 2)
    chip = me // 2

    loads = [
        pltpu.make_async_copy(ranks_in, ranks, load_sem.at[0]),
        pltpu.make_async_copy(sketch_one, s1, load_sem.at[1]),
    ] + [
        pltpu.make_async_copy(
            field.at[:, pl.ds(wide * h, wide)],
            flat.at[h, pl.ds(0, lines), :],
            load_sem.at[2 + h],
        )
        for h in range(2)
    ] + [
        pltpu.make_async_copy(sketch_two, s2, load_sem.at[4]),
    ]
    for load in loads:
        load.start()

    barrier = pltpu.get_barrier_semaphore()

    def greet(i, carry):
        peer = 2 * lax.rem(chip + 1 + i, chips) + 1
        pl.semaphore_signal(barrier, inc=1, device_id={"wide": peer}, device_id_type=MESH)
        return carry

    lax.fori_loop(0, chips - 1, greet, 0)
    leads = core == 1
    follows = core == 0
    twin = chip * 2 + 1 - core

    def nod():
        pl.semaphore_signal(note, inc=1, device_id={"wide": twin}, device_id_type=MESH)

    @pl.when(leads)
    def _():
        pl.semaphore_signal(barrier, inc=1, device_id={"wide": twin}, device_id_type=MESH)

    @pl.when(follows)
    def _():
        pl.semaphore_wait(barrier, 1)
        nod()

    bits = n.bit_length() - 1
    deltas = [(1 - 2 * lax.rem(me // (1 << b), 2)) * (1 << b) for b in range(bits)]

    def flipped(m):
        return me + sum(deltas[b] for b in range(bits) if (m >> b) & 1)

    alike = [(2 * m, flipped(2 * m)) for m in far_first(bits - 1, 2)]

    def copy(phase, source, target, peer):
        return pltpu.make_async_remote_copy(
            src_ref=source, dst_ref=target,
            send_sem=send_sem.at[phase], recv_sem=recv_sem.at[phase],
            device_id={"wide": peer}, device_id_type=MESH,
        )

    waits = []

    def later(phase, sent, when=None):
        def wait():
            copy(phase, sent, sent, twin).wait_send()

        waits.append(wait if when is None else functools.partial(pl.when(when), wait))

    def of_chip(c):
        return pl.ds(pl.multiple_of(c * rows, rows), rows)

    plane = me // PLANE
    below = me - plane * PLANE
    middle = jnp.logical_or(plane == 1, plane == 2)
    outside = jnp.logical_not(middle)
    slot = jnp.clip(me - PLANE, 0, 2 * PLANE - 1)
    holds = jnp.logical_and(middle, slot < holders)
    spare = jnp.logical_not(holds)
    turns = (7, 6, 5, 4, 3, 2, 1, 0)
    inside = [below + sum(deltas[b] for b in range(3) if (m >> b) & 1) for m in turns]
    nearer = jnp.where(plane < 2, PLANE, 2 * PLANE)
    farther = 3 * PLANE - nearer
    group = [b + farther for b in inside] + [b + nearer for b in inside[:-1]]
    edges = [b + 3 * (farther - PLANE) for b in inside] + [
        b + 3 * (nearer - PLANE) for b in inside
    ]

    for h in range(2):
        flat[h, lines:, :] = jnp.zeros((flat.shape[1] - lines, wide), jnp.float32)
    loads[0].wait()
    lane = lax.broadcasted_iota(jnp.int32, (1, size), 1)
    sub = lax.broadcasted_iota(jnp.int32, (size, 1), 0)
    keep_one = (lane < ranks[0]).astype(jnp.float32)
    keep_two = (lane < ranks[1]).astype(jnp.float32)
    loads[1].wait()
    turned = s1[...].T * (sub < ranks[0]).astype(jnp.float32)
    loads[2].wait()
    projected = mul(turned[:, :wide], flat[0, :lines, :], NT)
    loads[3].wait()
    projected = projected + mul(turned[:, wide:], flat[1, :lines, :], NT)
    part[1 - core] = mul(projected, flat[1 - core, pl.ds(0, lines), :], NN)

    @pl.when(leads)
    def _():
        pl.semaphore_wait(note, 1)

    copy(0, part.at[1 - core], pair, twin).start()
    later(0, pair)
    part[core] = mul(projected, flat[core, pl.ds(0, lines), :], NN)
    copy(0, pair, pair, twin).wait_recv()
    mine[...] = part[core] + pair[...]

    @pl.when(leads)
    def _():
        pl.semaphore_wait(barrier, n - 2)
        nod()

    @pl.when(follows)
    def _():
        pl.semaphore_wait(note, 1)

    for i, (m, peer) in enumerate(alike):
        copy(1, mine.at[of_chip(peer // 2), :], got.at[m // 2 - 1], peer).start()
    later(1, got)
    loads[4].wait()
    masked_two = (s2[...].T) * (sub < ranks[1]).astype(jnp.float32)
    s2t = masked_two
    copy(1, got, got, twin).wait_recv()
    full[core, of_chip(chip), :] = jnp.sum(got[...], axis=0) + mine[of_chip(chip), :]
    for m, peer in alike:
        own = full.at[core, of_chip(chip), :]
        copy(2, own, own, peer).start()
    later(2, got)
    copy(2, got, got, twin).wait_recv()
    copy(3, full.at[core], full.at[core], twin).start()
    later(3, pair)
    sk = full[core]
    rot[...] = mul(flat[core], sk, NT).reshape(rot.shape)
    inner = mul(sk, sk, NT)
    copy(3, pair, pair, twin).wait_recv()
    sk = full[1 - core]

    part_lines = PLANE * KB * ydev
    for base in (farther, nearer):
        first = base - PLANE
        ks = pl.ds(KB * first, KB * PLANE)
        span = pl.ds(pl.multiple_of(first * (KB * ydev), part_lines), part_lines)
        more = mul(flat[1 - core, span, :], sk, NT)
        rot[ks] = rot[ks] + more.reshape(KB * PLANE, ydev, size)
        for b in inside:
            peer = b + base
            j = peer - PLANE

            @pl.when(jnp.logical_and(j < holders, peer != me))
            def _():
                copy(
                    4, rot.at[pl.ds(KB * j, KB)], have.at[me], peer
                ).start()

    later(4, rot.at[pl.ds(0, KB * (holders - 1))], holds)
    later(4, rot.at[pl.ds(0, KB * holders)], spare)

    @pl.when(holds)
    def _():
        have[me] = rot[pl.ds(KB * slot, KB)]

    inner = inner + mul(sk, sk, NT)
    fill_work(work, inner, keep_one, size)
    inverse_factor(work, linv)

    @pl.when(holds)
    def _():
        everything = have.at[pl.ds(0, n - 1)]
        copy(4, everything, everything, twin).wait_recv()

    @pl.when(holds)
    def _():
        for k in range(KB):
            stack[k * size : (k + 1) * size, :] = mul(
                linv[...], have[:, k].reshape(n2, size), NT
            )
        mixed = stack[...]
        spread = mul(s2t, mixed, NT)
        total = mul(spread, mixed, NN)
        part_two[...] = total

    def of_slot(j):
        place = lax.rem(j, 2) * PLANE + j // 2
        return pl.ds(pl.multiple_of(place * rows, rows), rows)

    @pl.when(holds)
    def _():
        for peer in group:
            copy(6, part_two.at[of_slot(peer - PLANE), :], got_two.at[slot], peer).start()
        got_two[slot] = part_two[of_slot(slot), :]
        most = got_two.at[pl.ds(0, holders - 1)]
        copy(6, most, most, twin).wait_recv()

    @pl.when(jnp.logical_and(middle, spare))
    def _():
        copy(6, got_two, got_two, twin).wait_recv()

    later(6, part_two.at[pl.ds(0, size - rows), :], holds)
    most_two = full_two.at[pl.ds(0, size - rows), :]

    @pl.when(middle)
    def _():
        own = full_two.at[of_slot(slot), :]
        own[...] = jnp.sum(got_two[...], axis=0)
        for peer in group:
            copy(7, own, own, peer).start()
        for peer in edges:
            copy(5, own, own, peer).start()
        copy(7, most_two, most_two, twin).wait_recv()

    @pl.when(outside)
    def _():
        copy(5, full_two, full_two, twin).wait_recv()

    later(7, most_two, middle)
    later(5, full_two, middle)

    @pl.when(holds)
    def _():
        spun = mul(stack[...], full_two[...], NT)
        for d in range(n):
            for k in range(KB):
                give[d, k] = spun[k * size + per * d : k * size + per * (d + 1), :]
        for peer in edges + group:
            copy(8, give.at[peer], last.at[slot], peer).start()
        last[slot] = give[me]

    later(8, give.at[pl.ds(0, n - 1)], holds)
    sk = full_two[...]
    fill_work(work, mul(sk, sk, NT), keep_two, size)
    inverse_factor(work, linv)

    @pl.when(holds)
    def _():
        most = last.at[pl.ds(0, holders - 1)]
        copy(8, most, most, twin).wait_recv()

    @pl.when(spare)
    def _():
        copy(8, last, last, twin).wait_recv()

    done = mul(last[...].reshape(holders * KB * per, size), linv[...], NT)
    out[...] = done[: out.shape[0], :]

    for wait in waits:
        wait()


def fused(n, field, sketch_one, sketch_two, ranks):
    ydev, kdim, n1 = field.shape
    n2, size = sketch_two.shape
    chips = n // 2
    rows = size // chips
    wide = n1 // 2
    holders = -(-kdim // KB)
    padded = 2 * PLANE * KB
    per = size // n
    hbm = pl.BlockSpec(memory_space=pltpu.MemorySpace.HBM)
    f32 = jnp.float32
    lines = jnp.transpose(field, (1, 0, 2)).reshape(kdim * ydev, n1)
    core = pl.pallas_call(
        functools.partial(kernel, n),
        out_shape=pltpu.VMEM((kdim * per, size), f32),
        in_specs=[hbm, hbm, hbm, hbm],
        out_specs=pl.BlockSpec(memory_space=pltpu.VMEM),
        scratch_shapes=[
            pltpu.VMEM((2, padded * ydev, wide), f32),
            pltpu.VMEM((n1, size), f32),
            pltpu.VMEM((n2, size), f32),
            pltpu.SMEM((2,), jnp.int32),
            pltpu.VMEM((2, size, wide), f32),
            pltpu.VMEM((size, wide), f32),
            pltpu.VMEM((size, wide), f32),
            pltpu.VMEM((chips - 1, rows, wide), f32),
            pltpu.VMEM((2, size, wide), f32),
            pltpu.VMEM((padded, ydev, size), f32),
            pltpu.VMEM((n, KB, ydev, size), f32),
            pltpu.VMEM((size, 2 * size), f32),
            pltpu.VMEM((size, size), f32),
            pltpu.VMEM((KB * size, n2), f32),
            pltpu.VMEM((size, n2), f32),
            pltpu.VMEM((holders, rows, n2), f32),
            pltpu.VMEM((size, n2), f32),
            pltpu.VMEM((n, KB, per, size), f32),
            pltpu.VMEM((holders, KB, per, size), f32),
            pltpu.SemaphoreType.DMA((5,)),
            pltpu.SemaphoreType.DMA((9,)),
            pltpu.SemaphoreType.DMA((9,)),
            pltpu.SemaphoreType.REGULAR,
        ],
        compiler_params=pltpu.CompilerParams(
            collective_id=0, has_side_effects=True, vmem_limit_bytes=56 * 1024 * 1024
        ),
        cost_estimate=pl.CostEstimate(
            flops=600_000_000, bytes_accessed=2_000_000, transcendentals=256
        ),
    )(lines, sketch_one, sketch_two, ranks)
    return jnp.transpose(core.reshape(kdim, per, size), (1, 0, 2))


def solution(mesh):
    n = mesh.shape["wide"]

    def per_device(field, sketch_one, sketch_two, ranks):
        ydev, kdim, n1 = field.shape
        n2, size = sketch_two.shape
        fits = (
            mesh.shape["narrow"] == 1
            and size == 128
            and n == 32
            and ydev == 8
            and kdim <= 2 * PLANE * KB - KB
            and kdim > 2 * PLANE * KB - 2 * KB
            and n1 == 512
            and n2 == 8 * n
        )
        if fits:
            return fused(n, field, sketch_one, sketch_two, ranks)
        return general(field, sketch_one, sketch_two, ranks)

    return jax.shard_map(
        per_device,
        mesh=mesh,
        in_specs=(P("wide", "narrow", None), P(), P(), P()),
        out_specs=P("wide", "narrow", None),
        check_vma=False,
    )
```

```python
import functools

import jax
import jax.numpy as jnp
from jax import lax
from jax.experimental import pallas as pl
from jax.experimental.pallas import tpu as pltpu
from jax.sharding import PartitionSpec as P

HIGHEST = lax.Precision.HIGHEST
MESH = pl.DeviceIdType.MESH


def make_basis(local, sketch, rank):
    keep = (jnp.arange(sketch.shape[1]) < rank).astype(jnp.float32)
    masked = sketch * keep
    part = jnp.einsum("akn,ns->aks", local, masked, precision=HIGHEST)
    part = jnp.einsum("akn,aks->ns", local, part, precision=HIGHEST)
    sketched = lax.psum(part, ("wide", "narrow"))
    inner = jnp.dot(sketched.T, sketched, precision=HIGHEST) + jnp.diag(1.0 - keep)
    lower = jnp.linalg.cholesky(inner)
    return jax.scipy.linalg.solve_triangular(lower, sketched.T, lower=True)


def general(field, sketch_one, sketch_two, ranks):
    basis_one = make_basis(field, sketch_one, ranks[0])
    core_one = jnp.einsum("rn,ykn->rky", basis_one, field, precision=HIGHEST)
    regrouped = lax.all_to_all(core_one, "wide", split_axis=0, concat_axis=2, tiled=True)
    basis_two = make_basis(regrouped, sketch_two, ranks[1])
    return jnp.einsum("sn,rkn->rks", basis_two, regrouped, precision=HIGHEST)


def dot(a, b, dims):
    return lax.dot_general(
        a, b, (dims, ((), ())), precision=HIGHEST, preferred_element_type=jnp.float32
    )


def halves(x):
    high = x.astype(jnp.bfloat16)
    return high, (x - high.astype(jnp.float32)).astype(jnp.bfloat16)


def mul(a, b, dims):
    def one(x, y):
        return lax.dot_general(
            x, y, (dims, ((), ())), preferred_element_type=jnp.float32
        )

    (ah, al), (bh, bl) = halves(a), halves(b)
    rest = one(al, bh)
    if dims == NT and b.shape[1] == 128:
        joined = one(
            jnp.concatenate([ah, ah], axis=1), jnp.concatenate([bh, bl], axis=1)
        )
        return joined + rest
    if dims == NT and b.shape[0] == 128:
        joined = one(ah, jnp.concatenate([bh, bl], axis=0))
        return joined[:, :128] + (joined[:, 128:] + rest)
    return one(ah, bh) + (one(ah, bl) + rest)


NN = ((1,), (0,))
NT = ((1,), (1,))
TN = ((0,), (0,))
BLOCK = 8
TILES = 8
KB = 3
PLANE = 8


def inverse_factor(work, linv):
    size = linv.shape[0]
    tile = (BLOCK, size)
    group = TILES * BLOCK
    sub = lax.broadcasted_iota(jnp.int32, tile, 0)

    for r0 in range(0, size, group):
        own = work[r0 : r0 + group, :size]
        rest = work[r0 : r0 + group, size:]
        rows_a = [own[u * BLOCK : (u + 1) * BLOCK, :] for u in range(TILES)]
        rows_t = [rest[u * BLOCK : (u + 1) * BLOCK, :] for u in range(TILES)]
        panels_a, panels_t = [], []
        ahead = None
        for u in range(TILES):
            d, below = {}, {}
            for q in range(BLOCK):
                lane = r0 + u * BLOCK + q
                if ahead is None:
                    column = jnp.broadcast_to(rows_a[u][:, lane : lane + 1], tile)
                else:
                    column = ahead[q]
                for p in range(q, BLOCK):
                    d[p, q] = jnp.broadcast_to(column[p : p + 1, :], tile)
                for v in range(u + 1, TILES):
                    below[v, q] = jnp.broadcast_to(rows_a[v][:, lane : lane + 1], tile)
            ahead = None
            if u + 1 < TILES:
                first = r0 + (u + 1) * BLOCK
                ahead = [
                    jnp.broadcast_to(rows_a[u + 1][:, first + q : first + q + 1], tile)
                    for q in range(BLOCK)
                ]
            done_a, done_t = [], []
            panel_a = jnp.zeros(tile, jnp.float32)
            panel_t = jnp.zeros(tile, jnp.float32)
            for j in range(BLOCK):
                y = lax.rsqrt(d[j, j])
                for p in range(j + 1, BLOCK):
                    d[p, j] = d[p, j] * y
                for q in range(j + 1, BLOCK):
                    for p in range(q, BLOCK):
                        d[p, q] = d[p, q] - d[p, j] * d[q, j]
                for v in range(u + 1, TILES):
                    low = below[v, j] * y
                    below[v, j] = low
                    if v == u + 1:
                        for q in range(BLOCK):
                            across = jnp.broadcast_to(low[q : q + 1, :], tile)
                            ahead[q] = ahead[q] - low * across
                    for q in range(j + 1, BLOCK):
                        below[v, q] = below[v, q] - low * d[q, j]
                ra = jnp.broadcast_to(rows_a[u][j : j + 1, :], tile)
                rt = jnp.broadcast_to(rows_t[u][j : j + 1, :], tile)
                for k in range(j):
                    ra = ra - d[j, k] * done_a[k]
                    rt = rt - d[j, k] * done_t[k]
                ra = ra * y
                rt = rt * y
                done_a.append(ra)
                done_t.append(rt)
                panel_a = jnp.where(sub == j, ra, panel_a)
                panel_t = jnp.where(sub == j, rt, panel_t)
                for v in range(u + 1, TILES):
                    rows_a[v] = rows_a[v] - below[v, j] * ra
                    rows_t[v] = rows_t[v] - below[v, j] * rt
            panels_a.append(panel_a)
            panels_t.append(panel_t)
        panel_t = jnp.concatenate(panels_t, axis=0)
        panel_a = jnp.concatenate(panels_a, axis=0)
        linv[r0 : r0 + group, :] = panel_t
        end = r0 + group
        if end < size:
            both = jnp.concatenate([panel_a, panel_t], axis=1)
            work[end:, :] = work[end:, :] - dot(panel_a.T[end:, :], both, NN)


def fill_work(work, inner, keep_row, size):
    row = lax.broadcasted_iota(jnp.int32, (size, size), 0)
    col = lax.broadcasted_iota(jnp.int32, (size, size), 1)
    eye = (row == col).astype(jnp.float32)
    work[:, :size] = inner + eye * (1.0 - keep_row)
    work[:, size:] = eye


def far_first(bits, low):
    def hops(m):
        flat = sum((m >> b) & 1 for b in range(low))
        return flat + (m >> low)

    return sorted(range(1, 1 << bits), key=lambda m: -hops(m))


def kernel(
    n, field, sketch_one, sketch_two, ranks_in, out,
    flat, s1, s2, ranks, part, pair, mine, got, full, rot, have, work, linv, stack,
    part_two, got_two, full_two, give, last,
    load_sem, send_sem, recv_sem, note,
):
    me = lax.axis_index("wide")
    size = s1.shape[1]
    wide = flat.shape[2]
    holders = last.shape[0]
    lines = field.shape[0]
    ydev = rot.shape[1]
    n2 = s2.shape[0]
    per = size // n
    chips = n // 2
    rows = size // chips
    core = lax.rem(me, 2)
    chip = me // 2

    loads = [
        pltpu.make_async_copy(ranks_in, ranks, load_sem.at[0]),
        pltpu.make_async_copy(sketch_one, s1, load_sem.at[1]),
    ] + [
        pltpu.make_async_copy(
            field.at[:, pl.ds(wide * h, wide)],
            flat.at[h, pl.ds(0, lines), :],
            load_sem.at[2 + h],
        )
        for h in range(2)
    ] + [
        pltpu.make_async_copy(sketch_two, s2, load_sem.at[4]),
    ]
    for load in loads:
        load.start()

    barrier = pltpu.get_barrier_semaphore()

    def greet(i, carry):
        peer = 2 * lax.rem(chip + 1 + i, chips) + 1
        pl.semaphore_signal(barrier, inc=1, device_id={"wide": peer}, device_id_type=MESH)
        return carry

    lax.fori_loop(0, chips - 1, greet, 0)
    leads = core == 1
    follows = core == 0
    twin = chip * 2 + 1 - core

    def nod():
        pl.semaphore_signal(note, inc=1, device_id={"wide": twin}, device_id_type=MESH)

    @pl.when(leads)
    def _():
        pl.semaphore_signal(barrier, inc=1, device_id={"wide": twin}, device_id_type=MESH)

    @pl.when(follows)
    def _():
        pl.semaphore_wait(barrier, 1)
        nod()

    bits = n.bit_length() - 1
    deltas = [(1 - 2 * lax.rem(me // (1 << b), 2)) * (1 << b) for b in range(bits)]

    def flipped(m):
        return me + sum(deltas[b] for b in range(bits) if (m >> b) & 1)

    alike = [(2 * m, flipped(2 * m)) for m in far_first(bits - 1, 2)]

    def copy(phase, source, target, peer):
        return pltpu.make_async_remote_copy(
            src_ref=source, dst_ref=target,
            send_sem=send_sem.at[phase], recv_sem=recv_sem.at[phase],
            device_id={"wide": peer}, device_id_type=MESH,
        )

    waits = []

    def later(phase, sent, when=None):
        def wait():
            copy(phase, sent, sent, twin).wait_send()

        waits.append(wait if when is None else functools.partial(pl.when(when), wait))

    def of_chip(c):
        return pl.ds(pl.multiple_of(c * rows, rows), rows)

    plane = me // PLANE
    below = me - plane * PLANE
    middle = jnp.logical_or(plane == 1, plane == 2)
    outside = jnp.logical_not(middle)
    slot = jnp.clip(me - PLANE, 0, 2 * PLANE - 1)
    holds = jnp.logical_and(middle, slot < holders)
    spare = jnp.logical_not(holds)
    turns = (7, 6, 5, 4, 3, 2, 1, 0)
    inside = [below + sum(deltas[b] for b in range(3) if (m >> b) & 1) for m in turns]
    nearer = jnp.where(plane < 2, PLANE, 2 * PLANE)
    farther = 3 * PLANE - nearer
    group = [b + farther for b in inside] + [b + nearer for b in inside[:-1]]
    edges = [b + 3 * (farther - PLANE) for b in inside] + [
        b + 3 * (nearer - PLANE) for b in inside
    ]

    for h in range(2):
        flat[h, lines:, :] = jnp.zeros((flat.shape[1] - lines, wide), jnp.float32)
    loads[0].wait()
    lane = lax.broadcasted_iota(jnp.int32, (1, size), 1)
    sub = lax.broadcasted_iota(jnp.int32, (size, 1), 0)
    keep_one = (lane < ranks[0]).astype(jnp.float32)
    keep_two = (lane < ranks[1]).astype(jnp.float32)
    loads[1].wait()
    turned = s1[...].T * (sub < ranks[0]).astype(jnp.float32)
    loads[2].wait()
    projected = mul(turned[:, :wide], flat[0, :lines, :], NT)
    loads[3].wait()
    projected = projected + mul(turned[:, wide:], flat[1, :lines, :], NT)
    part[1 - core] = mul(projected, flat[1 - core, pl.ds(0, lines), :], NN)

    @pl.when(leads)
    def _():
        pl.semaphore_wait(note, 1)

    copy(0, part.at[1 - core], pair, twin).start()
    later(0, pair)
    part[core] = mul(projected, flat[core, pl.ds(0, lines), :], NN)
    copy(0, pair, pair, twin).wait_recv()
    mine[...] = part[core] + pair[...]

    @pl.when(leads)
    def _():
        pl.semaphore_wait(barrier, n - 2)
        nod()

    @pl.when(follows)
    def _():
        pl.semaphore_wait(note, 1)

    for i, (m, peer) in enumerate(alike):
        copy(1, mine.at[of_chip(peer // 2), :], got.at[m // 2 - 1], peer).start()
    later(1, got)
    loads[4].wait()
    masked_two = (s2[...].T) * (sub < ranks[1]).astype(jnp.float32)
    s2t = masked_two
    copy(1, got, got, twin).wait_recv()
    full[core, of_chip(chip), :] = jnp.sum(got[...], axis=0) + mine[of_chip(chip), :]
    for m, peer in alike:
        own = full.at[core, of_chip(chip), :]
        copy(2, own, own, peer).start()
    later(2, got)
    copy(2, got, got, twin).wait_recv()
    copy(3, full.at[core], full.at[core], twin).start()
    later(3, pair)
    sk = full[core]
    rot[...] = mul(flat[core], sk, NT).reshape(rot.shape)
    inner = mul(sk, sk, NT)
    copy(3, pair, pair, twin).wait_recv()
    sk = full[1 - core]

    part_lines = PLANE * KB * ydev
    for base in (farther, nearer):
        first = base - PLANE
        ks = pl.ds(KB * first, KB * PLANE)
        span = pl.ds(pl.multiple_of(first * (KB * ydev), part_lines), part_lines)
        more = mul(flat[1 - core, span, :], sk, NT)
        rot[ks] = rot[ks] + more.reshape(KB * PLANE, ydev, size)
        for b in inside:
            peer = b + base
            j = peer - PLANE

            @pl.when(jnp.logical_and(j < holders, peer != me))
            def _():
                copy(
                    4, rot.at[pl.ds(KB * j, KB)], have.at[me], peer
                ).start()

    later(4, rot.at[pl.ds(0, KB * (holders - 1))], holds)
    later(4, rot.at[pl.ds(0, KB * holders)], spare)

    @pl.when(holds)
    def _():
        have[me] = rot[pl.ds(KB * slot, KB)]

    inner = inner + mul(sk, sk, NT)
    fill_work(work, inner, keep_one, size)
    inverse_factor(work, linv)

    @pl.when(holds)
    def _():
        everything = have.at[pl.ds(0, n - 1)]
        copy(4, everything, everything, twin).wait_recv()

    @pl.when(holds)
    def _():
        for k in range(KB):
            stack[k * size : (k + 1) * size, :] = mul(
                linv[...], have[:, k].reshape(n2, size), NT
            )
        mixed = stack[...]
        spread = mul(s2t, mixed, NT)
        total = mul(spread, mixed, NN)
        part_two[...] = total

    def of_slot(j):
        place = lax.rem(j, 2) * PLANE + j // 2
        return pl.ds(pl.multiple_of(place * rows, rows), rows)

    @pl.when(holds)
    def _():
        for peer in group:
            copy(6, part_two.at[of_slot(peer - PLANE), :], got_two.at[slot], peer).start()
        got_two[slot] = part_two[of_slot(slot), :]
        most = got_two.at[pl.ds(0, holders - 1)]
        copy(6, most, most, twin).wait_recv()

    @pl.when(jnp.logical_and(middle, spare))
    def _():
        copy(6, got_two, got_two, twin).wait_recv()

    later(6, part_two.at[pl.ds(0, size - rows), :], holds)
    most_two = full_two.at[pl.ds(0, size - rows), :]

    @pl.when(middle)
    def _():
        own = full_two.at[of_slot(slot), :]
        own[...] = jnp.sum(got_two[...], axis=0)
        for peer in group:
            copy(7, own, own, peer).start()
        for peer in edges:
            copy(5, own, own, peer).start()
        copy(7, most_two, most_two, twin).wait_recv()

    @pl.when(outside)
    def _():
        copy(5, full_two, full_two, twin).wait_recv()

    later(7, most_two, middle)
    later(5, full_two, middle)

    @pl.when(holds)
    def _():
        spun = mul(stack[...], full_two[...], NT)
        for d in range(n):
            for k in range(KB):
                give[d, k] = spun[k * size + per * d : k * size + per * (d + 1), :]
        for peer in edges + group:
            copy(8, give.at[peer], last.at[slot], peer).start()
        last[slot] = give[me]

    later(8, give.at[pl.ds(0, n - 1)], holds)
    sk = full_two[...]
    fill_work(work, mul(sk, sk, NT), keep_two, size)
    inverse_factor(work, linv)

    @pl.when(holds)
    def _():
        most = last.at[pl.ds(0, holders - 1)]
        copy(8, most, most, twin).wait_recv()

    @pl.when(spare)
    def _():
        copy(8, last, last, twin).wait_recv()

    done = mul(last[...].reshape(holders * KB * per, size), linv[...], NT)
    out[...] = done[: out.shape[0], :]

    for wait in waits:
        wait()


def fused(n, field, sketch_one, sketch_two, ranks):
    ydev, kdim, n1 = field.shape
    n2, size = sketch_two.shape
    chips = n // 2
    rows = size // chips
    wide = n1 // 2
    holders = -(-kdim // KB)
    padded = 2 * PLANE * KB
    per = size // n
    hbm = pl.BlockSpec(memory_space=pltpu.MemorySpace.HBM)
    f32 = jnp.float32
    lines = jnp.transpose(field, (1, 0, 2)).reshape(kdim * ydev, n1)
    core = pl.pallas_call(
        functools.partial(kernel, n),
        out_shape=pltpu.VMEM((kdim * per, size), f32),
        in_specs=[hbm, hbm, hbm, hbm],
        out_specs=pl.BlockSpec(memory_space=pltpu.VMEM),
        scratch_shapes=[
            pltpu.VMEM((2, padded * ydev, wide), f32),
            pltpu.VMEM((n1, size), f32),
            pltpu.VMEM((n2, size), f32),
            pltpu.SMEM((2,), jnp.int32),
            pltpu.VMEM((2, size, wide), f32),
            pltpu.VMEM((size, wide), f32),
            pltpu.VMEM((size, wide), f32),
            pltpu.VMEM((chips - 1, rows, wide), f32),
            pltpu.VMEM((2, size, wide), f32),
            pltpu.VMEM((padded, ydev, size), f32),
            pltpu.VMEM((n, KB, ydev, size), f32),
            pltpu.VMEM((size, 2 * size), f32),
            pltpu.VMEM((size, size), f32),
            pltpu.VMEM((KB * size, n2), f32),
            pltpu.VMEM((size, n2), f32),
            pltpu.VMEM((holders, rows, n2), f32),
            pltpu.VMEM((size, n2), f32),
            pltpu.VMEM((n, KB, per, size), f32),
            pltpu.VMEM((holders, KB, per, size), f32),
            pltpu.SemaphoreType.DMA((5,)),
            pltpu.SemaphoreType.DMA((9,)),
            pltpu.SemaphoreType.DMA((9,)),
            pltpu.SemaphoreType.REGULAR,
        ],
        compiler_params=pltpu.CompilerParams(
            collective_id=0, has_side_effects=True, vmem_limit_bytes=56 * 1024 * 1024
        ),
        cost_estimate=pl.CostEstimate(
            flops=600_000_000, bytes_accessed=2_000_000, transcendentals=256
        ),
    )(lines, sketch_one, sketch_two, ranks)
    return jnp.transpose(core.reshape(kdim, per, size), (1, 0, 2))


def solution(mesh):
    n = mesh.shape["wide"]

    def per_device(field, sketch_one, sketch_two, ranks):
        ydev, kdim, n1 = field.shape
        n2, size = sketch_two.shape
        fits = (
            mesh.shape["narrow"] == 1
            and size == 128
            and n == 32
            and ydev == 8
            and kdim <= 2 * PLANE * KB - KB
            and kdim > 2 * PLANE * KB - 2 * KB
            and n1 == 512
            and n2 == 8 * n
        )
        if fits:
            return fused(n, field, sketch_one, sketch_two, ranks)
        return general(field, sketch_one, sketch_two, ranks)

    return jax.shard_map(
        per_device,
        mesh=mesh,
        in_specs=(P("wide", "narrow", None), P(), P(), P()),
        out_specs=P("wide", "narrow", None),
        check_vma=False,
    )
```

```python
import functools

import jax
import jax.numpy as jnp
from jax import lax
from jax.experimental import pallas as pl
from jax.experimental.pallas import tpu as pltpu
from jax.sharding import PartitionSpec as P

HIGHEST = lax.Precision.HIGHEST
MESH = pl.DeviceIdType.MESH


def make_basis(local, sketch, rank):
    keep = (jnp.arange(sketch.shape[1]) < rank).astype(jnp.float32)
    masked = sketch * keep
    part = jnp.einsum("akn,ns->aks", local, masked, precision=HIGHEST)
    part = jnp.einsum("akn,aks->ns", local, part, precision=HIGHEST)
    sketched = lax.psum(part, ("wide", "narrow"))
    inner = jnp.dot(sketched.T, sketched, precision=HIGHEST) + jnp.diag(1.0 - keep)
    lower = jnp.linalg.cholesky(inner)
    return jax.scipy.linalg.solve_triangular(lower, sketched.T, lower=True)


def general(field, sketch_one, sketch_two, ranks):
    basis_one = make_basis(field, sketch_one, ranks[0])
    core_one = jnp.einsum("rn,ykn->rky", basis_one, field, precision=HIGHEST)
    regrouped = lax.all_to_all(core_one, "wide", split_axis=0, concat_axis=2, tiled=True)
    basis_two = make_basis(regrouped, sketch_two, ranks[1])
    return jnp.einsum("sn,rkn->rks", basis_two, regrouped, precision=HIGHEST)


def dot(a, b, dims):
    return lax.dot_general(
        a, b, (dims, ((), ())), precision=HIGHEST, preferred_element_type=jnp.float32
    )


def halves(x):
    high = x.astype(jnp.bfloat16)
    return high, (x - high.astype(jnp.float32)).astype(jnp.bfloat16)


def mul(a, b, dims):
    def one(x, y):
        return lax.dot_general(
            x, y, (dims, ((), ())), preferred_element_type=jnp.float32
        )

    (ah, al), (bh, bl) = halves(a), halves(b)
    rest = one(al, bh)
    if dims == NT and b.shape[1] == 128:
        joined = one(
            jnp.concatenate([ah, ah], axis=1), jnp.concatenate([bh, bl], axis=1)
        )
        return joined + rest
    if dims == NT and b.shape[0] == 128:
        joined = one(ah, jnp.concatenate([bh, bl], axis=0))
        return joined[:, :128] + (joined[:, 128:] + rest)
    return one(ah, bh) + (one(ah, bl) + rest)


NN = ((1,), (0,))
NT = ((1,), (1,))
TN = ((0,), (0,))
BLOCK = 8
TILES = 4
KB = 3
PLANE = 8


def inverse_factor(work, linv):
    size = linv.shape[0]
    tile = (BLOCK, size)
    group = TILES * BLOCK
    sub = lax.broadcasted_iota(jnp.int32, tile, 0)

    for r0 in range(0, size, group):
        own = work[r0 : r0 + group, :size]
        rest = work[r0 : r0 + group, size:]
        rows_a = [own[u * BLOCK : (u + 1) * BLOCK, :] for u in range(TILES)]
        rows_t = [rest[u * BLOCK : (u + 1) * BLOCK, :] for u in range(TILES)]
        panels_a, panels_t = [], []
        ahead = None
        for u in range(TILES):
            d, below = {}, {}
            for q in range(BLOCK):
                lane = r0 + u * BLOCK + q
                if ahead is None:
                    column = jnp.broadcast_to(rows_a[u][:, lane : lane + 1], tile)
                else:
                    column = ahead[q]
                for p in range(q, BLOCK):
                    d[p, q] = jnp.broadcast_to(column[p : p + 1, :], tile)
                for v in range(u + 1, TILES):
                    below[v, q] = jnp.broadcast_to(rows_a[v][:, lane : lane + 1], tile)
            ahead = None
            if u + 1 < TILES:
                first = r0 + (u + 1) * BLOCK
                ahead = [
                    jnp.broadcast_to(rows_a[u + 1][:, first + q : first + q + 1], tile)
                    for q in range(BLOCK)
                ]
            done_a, done_t = [], []
            panel_a = jnp.zeros(tile, jnp.float32)
            panel_t = jnp.zeros(tile, jnp.float32)
            for j in range(BLOCK):
                y = lax.rsqrt(d[j, j])
                for p in range(j + 1, BLOCK):
                    d[p, j] = d[p, j] * y
                for q in range(j + 1, BLOCK):
                    for p in range(q, BLOCK):
                        d[p, q] = d[p, q] - d[p, j] * d[q, j]
                for v in range(u + 1, TILES):
                    low = below[v, j] * y
                    below[v, j] = low
                    if v == u + 1:
                        for q in range(BLOCK):
                            across = jnp.broadcast_to(low[q : q + 1, :], tile)
                            ahead[q] = ahead[q] - low * across
                    for q in range(j + 1, BLOCK):
                        below[v, q] = below[v, q] - low * d[q, j]
                ra = jnp.broadcast_to(rows_a[u][j : j + 1, :], tile)
                rt = jnp.broadcast_to(rows_t[u][j : j + 1, :], tile)
                for k in range(j):
                    ra = ra - d[j, k] * done_a[k]
                    rt = rt - d[j, k] * done_t[k]
                ra = ra * y
                rt = rt * y
                done_a.append(ra)
                done_t.append(rt)
                panel_a = jnp.where(sub == j, ra, panel_a)
                panel_t = jnp.where(sub == j, rt, panel_t)
                for v in range(u + 1, TILES):
                    rows_a[v] = rows_a[v] - below[v, j] * ra
                    rows_t[v] = rows_t[v] - below[v, j] * rt
            panels_a.append(panel_a)
            panels_t.append(panel_t)
        panel_t = jnp.concatenate(panels_t, axis=0)
        panel_a = jnp.concatenate(panels_a, axis=0)
        linv[r0 : r0 + group, :] = panel_t
        end = r0 + group
        if end < size:
            both = jnp.concatenate([panel_a, panel_t], axis=1)
            work[end:, :] = work[end:, :] - dot(panel_a.T[end:, :], both, NN)


def fill_work(work, inner, keep_row, size):
    row = lax.broadcasted_iota(jnp.int32, (size, size), 0)
    col = lax.broadcasted_iota(jnp.int32, (size, size), 1)
    eye = (row == col).astype(jnp.float32)
    work[:, :size] = inner + eye * (1.0 - keep_row)
    work[:, size:] = eye


def far_first(bits, low):
    def hops(m):
        flat = sum((m >> b) & 1 for b in range(low))
        return flat + (m >> low)

    return sorted(range(1, 1 << bits), key=lambda m: -hops(m))


def kernel(
    n, field, sketch_one, sketch_two, ranks_in, out,
    flat, s1, s2, ranks, part, pair, mine, got, full, rot, have, work, linv, stack,
    part_two, got_two, full_two, give, last,
    load_sem, send_sem, recv_sem, note,
):
    me = lax.axis_index("wide")
    size = s1.shape[1]
    wide = flat.shape[2]
    holders = last.shape[0]
    lines = field.shape[0]
    ydev = rot.shape[1]
    n2 = s2.shape[0]
    per = size // n
    chips = n // 2
    rows = size // chips
    core = lax.rem(me, 2)
    chip = me // 2

    loads = [
        pltpu.make_async_copy(ranks_in, ranks, load_sem.at[0]),
        pltpu.make_async_copy(sketch_one, s1, load_sem.at[1]),
    ] + [
        pltpu.make_async_copy(
            field.at[:, pl.ds(wide * h, wide)],
            flat.at[h, pl.ds(0, lines), :],
            load_sem.at[2 + h],
        )
        for h in range(2)
    ] + [
        pltpu.make_async_copy(sketch_two, s2, load_sem.at[4]),
    ]
    for load in loads:
        load.start()

    barrier = pltpu.get_barrier_semaphore()

    def greet(i, carry):
        peer = 2 * lax.rem(chip + 1 + i, chips) + 1
        pl.semaphore_signal(barrier, inc=1, device_id={"wide": peer}, device_id_type=MESH)
        return carry

    lax.fori_loop(0, chips - 1, greet, 0)
    leads = core == 1
    follows = core == 0
    twin = chip * 2 + 1 - core

    def nod():
        pl.semaphore_signal(note, inc=1, device_id={"wide": twin}, device_id_type=MESH)

    @pl.when(leads)
    def _():
        pl.semaphore_signal(barrier, inc=1, device_id={"wide": twin}, device_id_type=MESH)

    @pl.when(follows)
    def _():
        pl.semaphore_wait(barrier, 1)
        nod()

    bits = n.bit_length() - 1
    deltas = [(1 - 2 * lax.rem(me // (1 << b), 2)) * (1 << b) for b in range(bits)]

    def flipped(m):
        return me + sum(deltas[b] for b in range(bits) if (m >> b) & 1)

    alike = [(2 * m, flipped(2 * m)) for m in far_first(bits - 1, 2)]

    def copy(phase, source, target, peer):
        return pltpu.make_async_remote_copy(
            src_ref=source, dst_ref=target,
            send_sem=send_sem.at[phase], recv_sem=recv_sem.at[phase],
            device_id={"wide": peer}, device_id_type=MESH,
        )

    waits = []

    def later(phase, sent, when=None):
        def wait():
            copy(phase, sent, sent, twin).wait_send()

        waits.append(wait if when is None else functools.partial(pl.when(when), wait))

    def of_chip(c):
        return pl.ds(pl.multiple_of(c * rows, rows), rows)

    plane = me // PLANE
    below = me - plane * PLANE
    middle = jnp.logical_or(plane == 1, plane == 2)
    outside = jnp.logical_not(middle)
    slot = jnp.clip(me - PLANE, 0, 2 * PLANE - 1)
    holds = jnp.logical_and(middle, slot < holders)
    spare = jnp.logical_not(holds)
    turns = (7, 6, 5, 4, 3, 2, 1, 0)
    inside = [below + sum(deltas[b] for b in range(3) if (m >> b) & 1) for m in turns]
    nearer = jnp.where(plane < 2, PLANE, 2 * PLANE)
    farther = 3 * PLANE - nearer
    group = [b + farther for b in inside] + [b + nearer for b in inside[:-1]]
    edges = [b + 3 * (farther - PLANE) for b in inside] + [
        b + 3 * (nearer - PLANE) for b in inside
    ]

    for h in range(2):
        flat[h, lines:, :] = jnp.zeros((flat.shape[1] - lines, wide), jnp.float32)
    loads[0].wait()
    lane = lax.broadcasted_iota(jnp.int32, (1, size), 1)
    sub = lax.broadcasted_iota(jnp.int32, (size, 1), 0)
    keep_one = (lane < ranks[0]).astype(jnp.float32)
    keep_two = (lane < ranks[1]).astype(jnp.float32)
    loads[1].wait()
    turned = s1[...].T * (sub < ranks[0]).astype(jnp.float32)
    loads[2].wait()
    projected = mul(turned[:, :wide], flat[0, :lines, :], NT)
    loads[3].wait()
    projected = projected + mul(turned[:, wide:], flat[1, :lines, :], NT)
    part[1 - core] = mul(projected, flat[1 - core, pl.ds(0, lines), :], NN)

    @pl.when(leads)
    def _():
        pl.semaphore_wait(note, 1)

    copy(0, part.at[1 - core], pair, twin).start()
    later(0, pair)
    part[core] = mul(projected, flat[core, pl.ds(0, lines), :], NN)
    copy(0, pair, pair, twin).wait_recv()
    mine[...] = part[core] + pair[...]

    @pl.when(leads)
    def _():
        pl.semaphore_wait(barrier, n - 2)
        nod()

    @pl.when(follows)
    def _():
        pl.semaphore_wait(note, 1)

    for i, (m, peer) in enumerate(alike):
        copy(1, mine.at[of_chip(peer // 2), :], got.at[m // 2 - 1], peer).start()
    later(1, got)
    loads[4].wait()
    masked_two = (s2[...].T) * (sub < ranks[1]).astype(jnp.float32)
    s2t = masked_two
    copy(1, got, got, twin).wait_recv()
    full[core, of_chip(chip), :] = jnp.sum(got[...], axis=0) + mine[of_chip(chip), :]
    for m, peer in alike:
        own = full.at[core, of_chip(chip), :]
        copy(2, own, own, peer).start()
    later(2, got)
    copy(2, got, got, twin).wait_recv()
    copy(3, full.at[core], full.at[core], twin).start()
    later(3, pair)
    sk = full[core]
    rot[...] = mul(flat[core], sk, NT).reshape(rot.shape)
    inner = mul(sk, sk, NT)
    copy(3, pair, pair, twin).wait_recv()
    sk = full[1 - core]

    part_lines = PLANE * KB * ydev
    for base in (farther, nearer):
        first = base - PLANE
        ks = pl.ds(KB * first, KB * PLANE)
        span = pl.ds(pl.multiple_of(first * (KB * ydev), part_lines), part_lines)
        more = mul(flat[1 - core, span, :], sk, NT)
        rot[ks] = rot[ks] + more.reshape(KB * PLANE, ydev, size)
        for b in inside:
            peer = b + base
            j = peer - PLANE

            @pl.when(jnp.logical_and(j < holders, peer != me))
            def _():
                copy(
                    4, rot.at[pl.ds(KB * j, KB)], have.at[me], peer
                ).start()

    later(4, rot.at[pl.ds(0, KB * (holders - 1))], holds)
    later(4, rot.at[pl.ds(0, KB * holders)], spare)

    @pl.when(holds)
    def _():
        have[me] = rot[pl.ds(KB * slot, KB)]

    inner = inner + mul(sk, sk, NT)
    fill_work(work, inner, keep_one, size)
    inverse_factor(work, linv)

    @pl.when(holds)
    def _():
        everything = have.at[pl.ds(0, n - 1)]
        copy(4, everything, everything, twin).wait_recv()

    @pl.when(holds)
    def _():
        for k in range(KB):
            stack[k * size : (k + 1) * size, :] = mul(
                linv[...], have[:, k].reshape(n2, size), NT
            )
        mixed = stack[...]
        spread = mul(s2t, mixed, NT)
        total = mul(spread, mixed, NN)
        part_two[...] = total

    def of_slot(j):
        place = lax.rem(j, 2) * PLANE + j // 2
        return pl.ds(pl.multiple_of(place * rows, rows), rows)

    @pl.when(holds)
    def _():
        for peer in group:
            copy(6, part_two.at[of_slot(peer - PLANE), :], got_two.at[slot], peer).start()
        got_two[slot] = part_two[of_slot(slot), :]
        most = got_two.at[pl.ds(0, holders - 1)]
        copy(6, most, most, twin).wait_recv()

    @pl.when(jnp.logical_and(middle, spare))
    def _():
        copy(6, got_two, got_two, twin).wait_recv()

    later(6, part_two.at[pl.ds(0, size - rows), :], holds)
    most_two = full_two.at[pl.ds(0, size - rows), :]

    @pl.when(middle)
    def _():
        own = full_two.at[of_slot(slot), :]
        own[...] = jnp.sum(got_two[...], axis=0)
        for peer in group:
            copy(7, own, own, peer).start()
        for peer in edges:
            copy(5, own, own, peer).start()
        copy(7, most_two, most_two, twin).wait_recv()

    @pl.when(outside)
    def _():
        copy(5, full_two, full_two, twin).wait_recv()

    later(7, most_two, middle)
    later(5, full_two, middle)

    @pl.when(holds)
    def _():
        spun = mul(stack[...], full_two[...], NT)
        for d in range(n):
            for k in range(KB):
                give[d, k] = spun[k * size + per * d : k * size + per * (d + 1), :]
        for peer in edges + group:
            copy(8, give.at[peer], last.at[slot], peer).start()
        last[slot] = give[me]

    later(8, give.at[pl.ds(0, n - 1)], holds)
    sk = full_two[...]
    fill_work(work, mul(sk, sk, NT), keep_two, size)
    inverse_factor(work, linv)

    @pl.when(holds)
    def _():
        most = last.at[pl.ds(0, holders - 1)]
        copy(8, most, most, twin).wait_recv()

    @pl.when(spare)
    def _():
        copy(8, last, last, twin).wait_recv()

    done = mul(last[...].reshape(holders * KB * per, size), linv[...], NT)
    out[...] = done[: out.shape[0], :]

    for wait in waits:
        wait()


def fused(n, field, sketch_one, sketch_two, ranks):
    ydev, kdim, n1 = field.shape
    n2, size = sketch_two.shape
    chips = n // 2
    rows = size // chips
    wide = n1 // 2
    holders = -(-kdim // KB)
    padded = 2 * PLANE * KB
    per = size // n
    hbm = pl.BlockSpec(memory_space=pltpu.MemorySpace.HBM)
    f32 = jnp.float32
    lines = jnp.transpose(field, (1, 0, 2)).reshape(kdim * ydev, n1)
    core = pl.pallas_call(
        functools.partial(kernel, n),
        out_shape=pltpu.VMEM((kdim * per, size), f32),
        in_specs=[hbm, hbm, hbm, hbm],
        out_specs=pl.BlockSpec(memory_space=pltpu.VMEM),
        scratch_shapes=[
            pltpu.VMEM((2, padded * ydev, wide), f32),
            pltpu.VMEM((n1, size), f32),
            pltpu.VMEM((n2, size), f32),
            pltpu.SMEM((2,), jnp.int32),
            pltpu.VMEM((2, size, wide), f32),
            pltpu.VMEM((size, wide), f32),
            pltpu.VMEM((size, wide), f32),
            pltpu.VMEM((chips - 1, rows, wide), f32),
            pltpu.VMEM((2, size, wide), f32),
            pltpu.VMEM((padded, ydev, size), f32),
            pltpu.VMEM((n, KB, ydev, size), f32),
            pltpu.VMEM((size, 2 * size), f32),
            pltpu.VMEM((size, size), f32),
            pltpu.VMEM((KB * size, n2), f32),
            pltpu.VMEM((size, n2), f32),
            pltpu.VMEM((holders, rows, n2), f32),
            pltpu.VMEM((size, n2), f32),
            pltpu.VMEM((n, KB, per, size), f32),
            pltpu.VMEM((holders, KB, per, size), f32),
            pltpu.SemaphoreType.DMA((5,)),
            pltpu.SemaphoreType.DMA((9,)),
            pltpu.SemaphoreType.DMA((9,)),
            pltpu.SemaphoreType.REGULAR,
        ],
        compiler_params=pltpu.CompilerParams(
            collective_id=0, has_side_effects=True, vmem_limit_bytes=56 * 1024 * 1024
        ),
        cost_estimate=pl.CostEstimate(
            flops=600_000_000, bytes_accessed=2_000_000, transcendentals=256
        ),
    )(lines, sketch_one, sketch_two, ranks)
    return jnp.transpose(core.reshape(kdim, per, size), (1, 0, 2))


def solution(mesh):
    n = mesh.shape["wide"]

    def per_device(field, sketch_one, sketch_two, ranks):
        ydev, kdim, n1 = field.shape
        n2, size = sketch_two.shape
        fits = (
            mesh.shape["narrow"] == 1
            and size == 128
            and n == 32
            and ydev == 8
            and kdim <= 2 * PLANE * KB - KB
            and kdim > 2 * PLANE * KB - 2 * KB
            and n1 == 512
            and n2 == 8 * n
        )
        if fits:
            return fused(n, field, sketch_one, sketch_two, ranks)
        return general(field, sketch_one, sketch_two, ranks)

    return jax.shard_map(
        per_device,
        mesh=mesh,
        in_specs=(P("wide", "narrow", None), P(), P(), P()),
        out_specs=P("wide", "narrow", None),
        check_vma=False,
    )
```
